32 devices in a mesh: cohort: 2 (over x), ind: 16 (over z, y, core).
Axes of the slice: x: 2, y: 2, z: 4, core: 2. Of those that a mesh axis runs over, the one named last changes fastest.
Arguments:
- genotypes: bfloat16 [16384, 512], P(('cohort', 'ind')), parts along dimension 0, may hold values from -6 to 6
- phenotypes: bfloat16 [64, 16384], P(None, ('cohort', 'ind')), parts along dimension 1, may hold values from -6 to 6, as said below
- folds: int32 [16384], P(('cohort', 'ind')), parts along dimension 0, may hold values from 0 to 4
Outputs:
- block_predictions: float32 [5, 64, 16384], P(None, None, ('cohort', 'ind')), parts along dimension 2
- stacked_predictions: float32 [5, 64, 16384], P(None, None, ('cohort', 'ind')), parts along dimension 2
The draws below stay inside these ranges and needn't reach their ends.
There are 2 independent parts, one for each index of `cohort`. The reference program is written for one: setup_inputs(seed, part) draws one part's arguments, and reference() takes and returns one part's arrays. A program takes and returns all parts, laid end to end along the dimension named above; each array names one. Nothing has to cross between parts.
Inputs may be any that keep to these rules, and one draw needn't show every extreme that they name: `phenotypes`: trait values of mean about zero and variance about one.
All inputs are finite; a program needn't handle non-finite values.
Results may differ from the reference program's by a relative error of at most 0.0018.
Values may be sent and summed in bfloat16 or wider, within the bound.
A program may use at most 128 MiB of HBM per device.

```python
import jax
import jax.numpy as jnp
from jax import lax

VARIANTS = 512
TRAITS = 64
FOLDS = 5
RIDGES = 5
TOTAL = 8192


def genotype_parts(key):
    first, second = jax.random.split(key, 2)
    breaks = jax.random.randint(first, (2, TOTAL, VARIANTS), 0, 12)
    position = lax.broadcasted_iota(jnp.int32, (2, TOTAL, VARIANTS), 2)
    anchor = lax.cummax(jnp.where(breaks == 0, position, 0), axis=2)
    fresh = jax.random.randint(second, (2, TOTAL, VARIANTS), 0, 2)
    allele = jnp.take_along_axis(fresh, anchor, axis=2)
    dosage = jnp.sum(allele, axis=0).astype(jnp.float32)
    discrete = (dosage - 1.0) * 1.4142135
    return discrete


def draw_genotypes(key, part):
    discrete = genotype_parts(key)
    values = discrete
    return values.astype(jnp.bfloat16)


def draw_phenotypes(key, part):
    discrete = genotype_parts(key)
    key = jax.random.fold_in(key, 7)
    values = discrete
    first, second, third = jax.random.split(key, 3)
    causal = jax.random.randint(first, (TRAITS, 8), 0, VARIANTS)
    shares = jax.random.uniform(second, (TRAITS,), jnp.float32, 0.1, 0.8)
    genetic = jnp.sum(values[:, causal], axis=2) / jnp.sqrt(8.0)
    noise = jnp.clip(jax.random.normal(third, (TOTAL, TRAITS), jnp.float32), -4.0, 4.0)
    traits = jnp.sqrt(shares)[None, :] * genetic + jnp.sqrt(1.0 - shares)[None, :] * noise
    return jnp.transpose(jnp.clip(traits, -6.0, 6.0)).astype(jnp.bfloat16)


def touch_ends(array, own_key, low, high):
    shape = array.shape
    spot = [jax.random.randint(jax.random.fold_in(own_key, axis), (), 0, shape[axis]) for axis in range(len(shape))]
    array = array.at[tuple(spot)].set(low)
    longest = shape.index(max(shape))
    spot[longest] = (spot[longest] + 1) % shape[longest]
    return array.at[tuple(spot)].set(high)


def setup_inputs(seed: int = 0, part: int = 0) -> dict:
    key_list = jax.random.split(jax.random.key(seed), 4)
    part_keys = jax.random.split(jax.random.fold_in(key_list[3], part), 4)
    genotypes = draw_genotypes(jax.random.fold_in(jax.random.fold_in(key_list[3], part), 71), part)
    phenotypes = draw_phenotypes(jax.random.fold_in(jax.random.fold_in(key_list[3], part), 71), part)
    folds = touch_ends(jax.random.randint(part_keys[2], (TOTAL,), 0, FOLDS), jax.random.fold_in(part_keys[2], 1), 0, FOLDS - 1).astype(jnp.int32)
    return {"genotypes": genotypes, "phenotypes": phenotypes, "folds": folds}


heritability = (0.01, 0.25, 0.5, 0.75, 0.99)
epsilon = 1e-06

def ridge_values(count):
    shares = jnp.asarray(heritability, jnp.float32)
    return count * (1.0 - shares) / shares

def ridge_coefficients(gram, cross, count):
    leave_gram = lax.optimization_barrier(jnp.sum(gram, axis=0))[None] - gram
    leave_cross = lax.optimization_barrier(jnp.sum(cross, axis=0))[None] - cross
    identity = jnp.eye(gram.shape[1], dtype=jnp.float32)

    def one_ridge(ridge):
        lower = jnp.linalg.cholesky(leave_gram + ridge * identity[None])
        middle = jax.scipy.linalg.solve_triangular(lower, leave_cross, lower=True)
        return jax.scipy.linalg.solve_triangular(lower, middle, lower=True, trans=1)
    return lax.map(one_ridge, ridge_values(count))

def small_solve(matrix, rhs):
    size = matrix.shape[0]
    lower = {}
    for column in range(size):
        total = matrix[column, column]
        for inner in range(column):
            total = total - lower[column, inner] * lower[column, inner]
        lower[column, column] = jnp.sqrt(total)
        for row in range(column + 1, size):
            total = matrix[row, column]
            for inner in range(column):
                total = total - lower[row, inner] * lower[column, inner]
            lower[row, column] = total / lower[column, column]
    forward = []
    for row in range(size):
        total = rhs[row]
        for inner in range(row):
            total = total - lower[row, inner] * forward[inner]
        forward.append(total / lower[row, row])
    backward = {}
    for row in reversed(range(size)):
        total = forward[row]
        for inner in range(row + 1, size):
            total = total - lower[inner, row] * backward[inner]
        backward[row] = total / lower[row, row]
    return jnp.stack([backward[row] for row in range(size)])

def stack_weights(stack_gram, stack_cross, count):
    ridges = ridge_values(count)
    size = stack_gram.shape[1]
    identity = jnp.eye(size, dtype=jnp.float32)
    matrix = jnp.transpose(stack_gram, (1, 2, 0))[:, :, None, :] + ridges[None, None, :, None] * identity[:, :, None, None]
    rhs = jnp.broadcast_to(jnp.transpose(stack_cross)[:, None, :], (size, ridges.shape[0], stack_cross.shape[0]))
    return small_solve(matrix, rhs)

def stack_sums(block, phen):
    stack_gram = jnp.einsum('rpi,spi->prs', block, block, precision=lax.Precision.HIGHEST)
    stack_cross = jnp.einsum('rpi,pi->pr', block, phen, precision=lax.Precision.HIGHEST)
    return (stack_gram, stack_cross)

def combine_stack(weights, block):
    return jnp.einsum('rsp,rpi->spi', weights, block, precision=lax.Precision.HIGHEST)

def reference(genotypes, phenotypes, folds):
    count = genotypes.shape[0]
    grams = []
    crosses = []
    for fold in range(FOLDS):
        member = (folds == fold).astype(jnp.bfloat16)
        masked = genotypes * member[:, None]
        grams.append(jnp.dot(masked.T.astype(jnp.float32), genotypes.astype(jnp.float32), preferred_element_type=jnp.float32))
        crosses.append(jnp.dot(masked.T.astype(jnp.float32), phenotypes.T.astype(jnp.float32), preferred_element_type=jnp.float32))
    solved = ridge_coefficients(jnp.stack(grams), jnp.stack(crosses), count)
    coefficients = solved.astype(jnp.bfloat16)
    raw = jnp.zeros((RIDGES, TRAITS, count), jnp.float32)
    for fold in range(FOLDS):
        flat = jnp.transpose(coefficients[:, fold], (0, 2, 1)).reshape(RIDGES * TRAITS, VARIANTS)
        part = jnp.dot(flat.astype(jnp.float32), genotypes.T.astype(jnp.float32), preferred_element_type=jnp.float32).reshape(RIDGES, TRAITS, count)
        raw = jnp.where((folds == fold)[None, None, :], part, raw)
    squares = lax.optimization_barrier(jnp.sum(raw * raw, axis=2))
    block = raw / jnp.sqrt(squares / count + epsilon)[:, :, None]
    stack_gram, stack_cross = stack_sums(block, phenotypes.astype(jnp.float32))
    weights = stack_weights(stack_gram, stack_cross, count)
    return (block, combine_stack(weights, block))
```

```python
import functools

import jax
import jax.numpy as jnp
import numpy as np
from jax import lax
from jax.experimental import pallas as pl
from jax.experimental.pallas import tpu as pltpu
from jax.sharding import PartitionSpec as P

FOLDS = 5
RIDGES = 5
TILE = 128
GROUP = 8
EXTRA = 16

heritability = (0.01, 0.25, 0.5, 0.75, 0.99)
epsilon = 1e-06


def ridge_list(count):
    shares = np.asarray(heritability, np.float32)
    return [float(v) for v in np.float32(count) * (np.float32(1.0) - shares) / shares]


def plan(width):
    per_fold = min(width // FOLDS, RIDGES)
    slots = (RIDGES + per_fold - 1) // per_fold
    return per_fold, slots


def invert_tiles(tiles):
    lane = lax.broadcasted_iota(jnp.int32, (GROUP, TILE), 1)
    row = lax.broadcasted_iota(jnp.int32, (GROUP, TILE), 0)
    below = lax.broadcasted_iota(jnp.int32, (TILE - GROUP, TILE), 1) < GROUP

    def step(_, tiles):
        results = []
        for tile in tiles:
            head, rest = tile[:GROUP], tile[GROUP:]
            columns = [jnp.broadcast_to(head[:, j : j + 1], (GROUP, TILE)) for j in range(GROUP)]
            reduced = jnp.where(lane < GROUP, jnp.where(lane == row, 1.0, 0.0), head)
            for p in range(GROUP):
                column = columns[p]
                inverse = 1.0 / column[p : p + 1]
                here = row == p

                def eliminate(value):
                    pivot = jnp.broadcast_to(value[p : p + 1] * inverse, (GROUP, TILE))
                    return jnp.where(here, pivot, value - column * pivot)

                reduced = eliminate(reduced)
                for j in range(p + 1, GROUP):
                    columns[j] = eliminate(columns[j])
            total = jnp.where(below, 0.0, rest)
            for j in range(GROUP):
                total = total - jnp.broadcast_to(rest[:, j : j + 1], rest.shape) * reduced[j : j + 1]
            moved = jnp.concatenate([total, reduced], axis=0)
            results.append(pltpu.roll(moved, TILE - GROUP, 1))
        return tuple(results)

    return lax.fori_loop(0, TILE // GROUP, step, tuple(tiles))


def exact_dot(a, b):
    return lax.dot_general(
        a, b, (((1,), (0,)), ((), ())), precision=lax.Precision.HIGHEST, preferred_element_type=jnp.float32
    )


def solve_systems(total, work, out, ridges, slots, per_fold, me):
    size = total.shape[0]
    traits = total.shape[1] - size
    eye = lax.broadcasted_iota(jnp.int32, (size, size), 0) == lax.broadcasted_iota(jnp.int32, (size, size), 1)
    for s in range(slots):
        level = lax.rem(lax.rem(me, per_fold) * slots + s, RIDGES)
        ridge = jnp.float32(ridges[0])
        for r in range(1, RIDGES):
            ridge = jnp.where(level == r, jnp.float32(ridges[r]), ridge)
        work[s, :, :size] = total[:, :size] + jnp.where(eye, ridge, 0.0)
        work[s, :, size:] = total[:, size:]
    for first in range(0, size, TILE):
        last = first + TILE
        inverses = invert_tiles([work[s, first:last, first:last] for s in range(slots)])
        for s in range(slots):
            scaled = exact_dot(inverses[s], work[s, first:last, last:])
            if first:
                work[s, :first, last:] = work[s, :first, last:] - exact_dot(work[s, :first, first:last], scaled)
            if last < size:
                work[s, last:, last:] = work[s, last:, last:] - exact_dot(work[s, last:, first:last], scaled)
            work[s, first:last, last:] = scaled
    for s in range(slots):
        out[s] = work[s, :, size:].T.astype(out.dtype)


def fit_kernel(width, ridges, per_fold, slots, blocks, out, total, work):
    step = pl.program_id(0)
    me = lax.axis_index("ind")
    size = total.shape[0]
    fold = jnp.minimum(me // per_fold, FOLDS - 1).astype(jnp.float32)
    rows = total.shape[1]

    @pl.when(step == 0)
    def _():
        total[...] = jnp.zeros_like(total)

    keep = (blocks[0, rows : rows + 1, :].astype(jnp.float32) != fold).astype(jnp.bfloat16)
    total[...] += lax.dot_general(
        blocks[0, :size, :] * keep,
        blocks[0, :rows, :],
        (((1,), (1,)), ((), ())),
        preferred_element_type=jnp.float32,
    )

    @pl.when(step == width - 1)
    def _():
        solve_systems(total, work, out, ridges, slots, per_fold, me)


def fit(blocks, size, traits, ridges):
    width, rows, individuals = blocks.shape
    per_fold, slots = plan(width)
    return pl.pallas_call(
        functools.partial(fit_kernel, width, ridges, per_fold, slots),
        grid=(width,),
        in_specs=[pl.BlockSpec((1, rows, individuals), lambda i: (i, 0, 0))],
        out_specs=pl.BlockSpec((slots, traits, size), lambda i: (0, 0, 0)),
        out_shape=jax.ShapeDtypeStruct((slots, traits, size), jnp.bfloat16),
        scratch_shapes=[
            pltpu.VMEM((size, size + traits), jnp.float32),
            pltpu.VMEM((slots, size, size + traits), jnp.float32),
        ],
        compiler_params=pltpu.CompilerParams(vmem_limit_bytes=40 << 20),
    )(blocks)


def small_solve(matrix, rhs):
    size = len(rhs)
    lower = {}
    for column in range(size):
        total = matrix[column][column]
        for inner in range(column):
            total = total - lower[column, inner] * lower[column, inner]
        lower[column, column] = jnp.sqrt(total)
        for row in range(column + 1, size):
            total = matrix[row][column]
            for inner in range(column):
                total = total - lower[row, inner] * lower[column, inner]
            lower[row, column] = total / lower[column, column]
    forward = []
    for row in range(size):
        total = rhs[row]
        for inner in range(row):
            total = total - lower[row, inner] * forward[inner]
        forward.append(total / lower[row, row])
    backward = {}
    for row in reversed(range(size)):
        total = forward[row]
        for inner in range(row + 1, size):
            total = total - lower[inner, row] * backward[inner]
        backward[row] = total / lower[row, row]
    return [backward[row] for row in range(size)]


def predict_kernel(per_fold, slots, coefficients, block, raw, sums):
    traits, size = coefficients.shape[2:]
    rows = size + traits
    geno = block[:size, :]
    phen = block[size:rows, :].astype(jnp.float32)
    folds = block[rows : rows + 1, :].astype(jnp.float32)
    total = None
    for fold in range(FOLDS):
        masked = geno * (folds == float(fold)).astype(jnp.bfloat16)
        flat = jnp.concatenate(
            [coefficients[fold * per_fold + r // slots, r % slots] for r in range(RIDGES)], axis=0
        )
        part = lax.dot_general(flat, masked, (((1,), (0,)), ((), ())), preferred_element_type=jnp.float32)
        total = part if total is None else total + part
    raw[...] = total
    parts = [total[r * traits : (r + 1) * traits] for r in range(RIDGES)]
    lane = lax.broadcasted_iota(jnp.int32, (traits, TILE), 1)
    packed = jnp.zeros((traits, TILE), jnp.float32)
    place = 0
    for r in range(RIDGES):
        for other in parts[: r + 1] + [phen]:
            packed = jnp.where(lane == place, jnp.sum(parts[r] * other, axis=1, keepdims=True), packed)
            place += 1
    sums[...] = packed


def finish_kernel(count, ridges, sums, raw, block, stacked):
    traits = sums.shape[0]
    gram = {}
    cross = []
    place = 0
    for r in range(RIDGES):
        for s in range(r + 1):
            gram[r, s] = sums[:, place : place + 1]
            place += 1
        cross.append(sums[:, place : place + 1])
        place += 1
    scale = [1.0 / jnp.sqrt(gram[r, r] / count + epsilon) for r in range(RIDGES)]
    lane = lax.broadcasted_iota(jnp.int32, (traits, TILE), 1)
    ridge = jnp.full((traits, TILE), ridges[0], jnp.float32)
    for s in range(1, RIDGES):
        ridge = jnp.where(lane == s, ridges[s], ridge)
    matrix = [
        [
            jnp.broadcast_to(gram[r, s] * scale[r] * scale[s], (traits, TILE)) + (ridge if r == s else 0.0)
            if s <= r
            else None
            for s in range(RIDGES)
        ]
        for r in range(RIDGES)
    ]
    rhs = [jnp.broadcast_to(cross[r] * scale[r], (traits, TILE)) for r in range(RIDGES)]
    weights = small_solve(matrix, rhs)
    parts = []
    for r in range(RIDGES):
        part = raw[r * traits : (r + 1) * traits, :] * scale[r]
        block[r] = part
        parts.append(part)
    for s in range(RIDGES):
        total = weights[0][:, s : s + 1] * parts[0]
        for r in range(1, RIDGES):
            total = total + weights[r][:, s : s + 1] * parts[r]
        stacked[s] = total


def shards(genotypes, phenotypes, folds):
    rows, size = genotypes.shape
    traits = phenotypes.shape[0]
    width = lax.axis_size("ind")
    count = rows * width
    ridges = ridge_list(count)
    per_fold, slots = plan(width)
    own = jnp.concatenate(
        [genotypes.T, phenotypes, jnp.broadcast_to(folds.astype(jnp.bfloat16)[None], (EXTRA, rows))], axis=0
    )
    blocks = lax.all_gather(own, "ind", axis=0)
    solved = fit(blocks, size, traits, ridges)
    coefficients = lax.all_gather(solved, "ind", axis=0)
    raw, sums = pl.pallas_call(
        functools.partial(predict_kernel, per_fold, slots),
        out_shape=(
            jax.ShapeDtypeStruct((RIDGES * traits, rows), jnp.float32),
            jax.ShapeDtypeStruct((traits, TILE), jnp.float32),
        ),
        compiler_params=pltpu.CompilerParams(vmem_limit_bytes=40 << 20),
    )(coefficients, own)
    sums = lax.psum(sums, "ind")
    shape = jax.ShapeDtypeStruct((RIDGES, traits, rows), jnp.float32)
    return pl.pallas_call(
        functools.partial(finish_kernel, count, ridges),
        out_shape=(shape, shape),
        compiler_params=pltpu.CompilerParams(vmem_limit_bytes=40 << 20),
    )(sums, raw)


def solution(mesh):
    placed = (P(("cohort", "ind"), None), P(None, ("cohort", "ind")), P(("cohort", "ind")))
    return jax.shard_map(
        shards,
        mesh=mesh,
        in_specs=placed,
        out_specs=(P(None, None, ("cohort", "ind")), P(None, None, ("cohort", "ind"))),
        check_vma=False,
    )
```

```python
import functools

import jax
import jax.numpy as jnp
import numpy as np
from jax import lax
from jax.experimental import pallas as pl
from jax.experimental.pallas import tpu as pltpu
from jax.sharding import PartitionSpec as P

FOLDS = 5
RIDGES = 5
TILE = 128
GROUP = 8
EXTRA = 16

heritability = (0.01, 0.25, 0.5, 0.75, 0.99)
epsilon = 1e-06


def ridge_list(count):
    shares = np.asarray(heritability, np.float32)
    return [float(v) for v in np.float32(count) * (np.float32(1.0) - shares) / shares]


def plan(width):
    per_fold = min(width // FOLDS, RIDGES)
    slots = (RIDGES + per_fold - 1) // per_fold
    return per_fold, slots


def invert_tiles(tiles):
    lane = lax.broadcasted_iota(jnp.int32, (GROUP, TILE), 1)
    row = lax.broadcasted_iota(jnp.int32, (GROUP, TILE), 0)
    below = lax.broadcasted_iota(jnp.int32, (TILE - GROUP, TILE), 1) < GROUP

    def step(_, tiles):
        results = []
        for tile in tiles:
            head, rest = tile[:GROUP], tile[GROUP:]
            columns = [jnp.broadcast_to(head[:, j : j + 1], (GROUP, TILE)) for j in range(GROUP)]
            reduced = jnp.where(lane < GROUP, jnp.where(lane == row, 1.0, 0.0), head)
            for p in range(GROUP):
                column = columns[p]
                inverse = 1.0 / column[p : p + 1]
                here = row == p

                def eliminate(value):
                    pivot = jnp.broadcast_to(value[p : p + 1] * inverse, (GROUP, TILE))
                    return jnp.where(here, pivot, value - column * pivot)

                reduced = eliminate(reduced)
                for j in range(p + 1, GROUP):
                    columns[j] = eliminate(columns[j])
            total = jnp.where(below, 0.0, rest)
            for j in range(GROUP):
                total = total - jnp.broadcast_to(rest[:, j : j + 1], rest.shape) * reduced[j : j + 1]
            moved = jnp.concatenate([total, reduced], axis=0)
            results.append(pltpu.roll(moved, TILE - GROUP, 1))
        return tuple(results)

    return lax.fori_loop(0, TILE // GROUP, step, tuple(tiles))


def exact_dot(a, b):
    return lax.dot_general(
        a, b, (((1,), (0,)), ((), ())), precision=lax.Precision.HIGHEST, preferred_element_type=jnp.float32
    )


def solve_systems(total, work, out, ridges, slots, per_fold, me):
    size = total.shape[0]
    traits = total.shape[1] - size
    eye = lax.broadcasted_iota(jnp.int32, (size, size), 0) == lax.broadcasted_iota(jnp.int32, (size, size), 1)
    for s in range(slots):
        level = lax.rem(lax.rem(me, per_fold) * slots + s, RIDGES)
        ridge = jnp.float32(ridges[0])
        for r in range(1, RIDGES):
            ridge = jnp.where(level == r, jnp.float32(ridges[r]), ridge)
        work[s, :, :size] = total[:, :size] + jnp.where(eye, ridge, 0.0)
        work[s, :, size:] = total[:, size:]
    for first in range(0, size, TILE):
        last = first + TILE
        inverses = invert_tiles([work[s, first:last, first:last] for s in range(slots)])
        for s in range(slots):
            scaled = exact_dot(inverses[s], work[s, first:last, last:])
            if first:
                work[s, :first, last:] = work[s, :first, last:] - exact_dot(work[s, :first, first:last], scaled)
            if last < size:
                work[s, last:, last:] = work[s, last:, last:] - exact_dot(work[s, last:, first:last], scaled)
            work[s, first:last, last:] = scaled
    for s in range(slots):
        out[s] = work[s, :, size:].T.astype(out.dtype)


def layout(width):
    across = 2 if width == 16 else 1
    return width // (2 * across), across


def index_of(z, y, core, across):
    return (z * across + y) * 2 + core


def place_of(me, across):
    return me // (2 * across), lax.rem(me // 2, across), lax.rem(me, 2)


def copy_to(source, target, send, receive, device):
    return pltpu.make_async_remote_copy(
        src_ref=source,
        dst_ref=target,
        send_sem=send,
        recv_sem=receive,
        device_id={"ind": device},
        device_id_type=pl.DeviceIdType.MESH,
    )


def greet(partners):
    barrier = pltpu.get_barrier_semaphore()
    for exists, device in partners:

        @pl.when(exists)
        def _(device=device):
            pl.semaphore_signal(
                barrier, inc=1, device_id={"ind": device}, device_id_type=pl.DeviceIdType.MESH
            )

    expected = jnp.int32(0)
    for exists, _ in partners:
        expected = expected + exists.astype(jnp.int32)
    pl.semaphore_wait(barrier, expected)


UP, DOWN, ACROSS, SIBLING = range(4)


def spread(blocks, send, receive, width, use):
    depth, across = layout(width)
    me = lax.axis_index("ind")
    z, y, core = place_of(me, across)
    sibling = index_of(z, y, 1 - core, across)
    opposite = index_of(z, lax.rem(y + 1, across), core, across)

    def copy(index, way):
        device = {
            UP: index_of(z + 1, y, core, across),
            DOWN: index_of(z - 1, y, core, across),
            ACROSS: opposite,
            SIBLING: sibling,
        }[way]
        return copy_to(blocks.at[index], blocks.at[index], send.at[way, index], receive.at[index], device)

    def arrived(index):
        copy(index, SIBLING).wait_recv()

    def line(step, side):
        origin = z + (2 * side - 1) * step
        valid = (step >= 0) & (origin >= 0) & (origin < depth) & ((step > 0) | (side == 0))
        return origin, valid

    def body(step, carry):
        for side in (0, 1):
            origin, valid = line(step, side)
            index = index_of(origin, y, core, across)

            @pl.when(valid)
            def _(index=index, side=side):
                @pl.when(step > 0)
                def _():
                    arrived(index)

                @pl.when((z < depth - 1) if side == 0 else (z > 0))
                def _():
                    copy(index, UP if side == 0 else DOWN).start()

                if side == 0:

                    @pl.when((step == 0) & (z > 0))
                    def _():
                        copy(index, DOWN).start()

                if across > 1:
                    copy(index, ACROSS).start()
                copy(index, SIBLING).start()

        if across > 1:
            for side in (0, 1):
                origin, valid = line(step - 1, side)
                index = index_of(origin, 1 - y, core, across)

                @pl.when(valid)
                def _(index=index):
                    arrived(index)
                    copy(index, SIBLING).start()

        def visit(turn, inner):
            side = lax.rem(turn, 2)
            crossed = lax.rem(turn // 2, across)
            shared = turn // (2 * across)
            origin, valid = line(step - crossed - shared, side)
            there = lax.rem(y + crossed, across)
            index = index_of(origin, there, lax.rem(core + shared, 2), across)

            @pl.when(valid)
            def _():
                @pl.when(shared == 1)
                def _():
                    arrived(index)

                use(index)

            return inner

        return lax.fori_loop(0, 4 * across, visit, carry)

    lax.fori_loop(0, depth + across, body, 0)

    def settle(origin, carry):
        own = index_of(origin, y, core, across)

        @pl.when((z < depth - 1) & (origin <= z))
        def _():
            copy(own, UP).wait_send()

        @pl.when((z > 0) & (origin >= z))
        def _():
            copy(own, DOWN).wait_send()

        copy(own, SIBLING).wait_send()
        if across > 1:
            copy(own, ACROSS).wait_send()
            copy(index_of(origin, 1 - y, core, across), SIBLING).wait_send()
        return carry

    lax.fori_loop(0, depth, settle, 0)


def spread_partners(width):
    depth, across = layout(width)
    me = lax.axis_index("ind")
    z, y, core = place_of(me, across)
    partners = [
        (z < depth - 1, index_of(z + 1, y, core, across)),
        (z > 0, index_of(z - 1, y, core, across)),
        (z >= 0, index_of(z, y, 1 - core, across)),
    ]
    if across > 1:
        partners.append((z >= 0, index_of(z, 1 - y, core, across)))
    return partners


def gram_kernel(width, per_fold, own, total, blocks, send, receive, local):
    me = lax.axis_index("ind")
    rows, size = total.shape[1], total.shape[0]
    fold = jnp.minimum(me // per_fold, FOLDS - 1).astype(jnp.float32)
    fill = pltpu.make_async_copy(own, blocks.at[me], local)
    fill.start()
    greet(spread_partners(width))
    total[...] = jnp.zeros_like(total)
    fill.wait()

    def use(index):
        keep = (blocks[index, rows : rows + EXTRA, :].astype(jnp.float32)[:1] != fold).astype(jnp.bfloat16)
        total[...] += lax.dot_general(
            blocks[index, :size, :] * keep,
            blocks[index, :rows, :],
            (((1,), (1,)), ((), ())),
            preferred_element_type=jnp.float32,
        )

    spread(blocks, send, receive, width, use)


def leave_gram(own, width, size, traits):
    rows, individuals = own.shape
    per_fold, _ = plan(width)
    return pl.pallas_call(
        functools.partial(gram_kernel, width, per_fold),
        out_shape=jax.ShapeDtypeStruct((size, size + traits), jnp.float32),
        in_specs=[pl.BlockSpec(memory_space=pl.ANY)],
        out_specs=pl.BlockSpec(memory_space=pltpu.VMEM),
        scratch_shapes=[
            pltpu.VMEM((width, rows, individuals), jnp.bfloat16),
            pltpu.SemaphoreType.DMA((4, width)),
            pltpu.SemaphoreType.DMA((width,)),
            pltpu.SemaphoreType.DMA,
        ],
        compiler_params=pltpu.CompilerParams(
            collective_id=0,
            has_side_effects=True,
            vmem_limit_bytes=(12 << 20) + 2 * width * rows * individuals,
        ),
    )(own)


def fit_kernel(ridges, per_fold, slots, total, out, work):
    solve_systems(total, work, out, ridges, slots, per_fold, lax.axis_index("ind"))


def fit(total, ridges, width):
    per_fold, slots = plan(width)
    size = total.shape[0]
    traits = total.shape[1] - size
    return pl.pallas_call(
        functools.partial(fit_kernel, ridges, per_fold, slots),
        out_shape=jax.ShapeDtypeStruct((slots, traits, size), jnp.bfloat16),
        scratch_shapes=[pltpu.VMEM((slots, size, size + traits), jnp.float32)],
        compiler_params=pltpu.CompilerParams(vmem_limit_bytes=40 << 20),
    )(total)


def small_solve(matrix, rhs):
    size = len(rhs)
    lower = {}
    for column in range(size):
        total = matrix[column][column]
        for inner in range(column):
            total = total - lower[column, inner] * lower[column, inner]
        lower[column, column] = jnp.sqrt(total)
        for row in range(column + 1, size):
            total = matrix[row][column]
            for inner in range(column):
                total = total - lower[row, inner] * lower[column, inner]
            lower[row, column] = total / lower[column, column]
    forward = []
    for row in range(size):
        total = rhs[row]
        for inner in range(row):
            total = total - lower[row, inner] * forward[inner]
        forward.append(total / lower[row, row])
    backward = {}
    for row in reversed(range(size)):
        total = forward[row]
        for inner in range(row + 1, size):
            total = total - lower[inner, row] * backward[inner]
        backward[row] = total / lower[row, row]
    return [backward[row] for row in range(size)]


def predict_kernel(
    width, per_fold, slots, solved, block, raw, sums,
    coefficients, near, far, send, receive, near_send, near_receive, far_send, far_receive,
):
    traits, size = coefficients.shape[2:]
    rows = size + traits
    depth, across = layout(width)
    me = lax.axis_index("ind")
    z, y, core = place_of(me, across)
    corner = y * 2 + core
    near_devices = [(lax.rem(corner + k, 2 * across), k) for k in range(1, 2 * across)]
    far_devices = [(lax.rem(z + k, depth), k) for k in range(1, depth)]
    always = me >= 0
    coefficients[me] = solved[...]
    greet(
        [(always, z * 2 * across + other) for other, _ in near_devices]
        + [(always, other * 2 * across + corner) for other, _ in far_devices]
    )
    spread(coefficients, send, receive, width, lambda index: None)
    geno = block[:size, :]
    phen = block[size:rows, :].astype(jnp.float32)
    folds = block[rows : rows + 1, :].astype(jnp.float32)
    total = None
    for fold in range(FOLDS):
        masked = geno * (folds == float(fold)).astype(jnp.bfloat16)
        flat = jnp.concatenate(
            [coefficients[fold * per_fold + r // slots, r % slots] for r in range(RIDGES)], axis=0
        )
        part = lax.dot_general(flat, masked, (((1,), (0,)), ((), ())), preferred_element_type=jnp.float32)
        total = part if total is None else total + part
    raw[...] = total
    parts = [total[r * traits : (r + 1) * traits] for r in range(RIDGES)]
    lane = lax.broadcasted_iota(jnp.int32, (traits, TILE), 1)
    packed = jnp.zeros((traits, TILE), jnp.float32)
    place = 0
    for r in range(RIDGES):
        for other in parts[: r + 1] + [phen]:
            packed = jnp.where(lane == place, jnp.sum(parts[r] * other, axis=1, keepdims=True), packed)
            place += 1

    def exchange(buffer, mine, devices, sends, receives, device_of):
        copies = []
        for other, k in devices:
            copy = copy_to(
                buffer.at[mine], buffer.at[mine], sends.at[k], receives.at[mine], device_of(other)
            )
            copy.start()
            copies.append(copy)
        for other, k in devices:
            copy_to(
                buffer.at[other], buffer.at[other], sends.at[k], receives.at[other], device_of(other)
            ).wait_recv()
        for copy in copies:
            copy.wait_send()

    near[corner] = packed
    exchange(near, corner, near_devices, near_send, near_receive, lambda other: z * 2 * across + other)
    far[z] = jnp.sum(near[...], axis=0)
    exchange(far, z, far_devices, far_send, far_receive, lambda other: other * 2 * across + corner)
    sums[...] = jnp.sum(far[...], axis=0)


def predict(solved, own, width):
    slots, traits, size = solved.shape
    per_fold, _ = plan(width)
    depth, across = layout(width)
    return pl.pallas_call(
        functools.partial(predict_kernel, width, per_fold, slots),
        out_shape=(
            jax.ShapeDtypeStruct((RIDGES * traits, own.shape[1]), jnp.float32),
            jax.ShapeDtypeStruct((traits, TILE), jnp.float32),
        ),
        scratch_shapes=[
            pltpu.VMEM((width, slots, traits, size), jnp.bfloat16),
            pltpu.VMEM((2 * across, traits, TILE), jnp.float32),
            pltpu.VMEM((depth, traits, TILE), jnp.float32),
            pltpu.SemaphoreType.DMA((4, width)),
            pltpu.SemaphoreType.DMA((width,)),
            pltpu.SemaphoreType.DMA((2 * across,)),
            pltpu.SemaphoreType.DMA((2 * across,)),
            pltpu.SemaphoreType.DMA((depth,)),
            pltpu.SemaphoreType.DMA((depth,)),
        ],
        compiler_params=pltpu.CompilerParams(
            collective_id=1, has_side_effects=True, vmem_limit_bytes=40 << 20
        ),
    )(solved, own)


def finish_kernel(count, ridges, sums, raw, block, stacked):
    traits = sums.shape[0]
    gram = {}
    cross = []
    place = 0
    for r in range(RIDGES):
        for s in range(r + 1):
            gram[r, s] = sums[:, place : place + 1]
            place += 1
        cross.append(sums[:, place : place + 1])
        place += 1
    scale = [1.0 / jnp.sqrt(gram[r, r] / count + epsilon) for r in range(RIDGES)]
    lane = lax.broadcasted_iota(jnp.int32, (traits, TILE), 1)
    ridge = jnp.full((traits, TILE), ridges[0], jnp.float32)
    for s in range(1, RIDGES):
        ridge = jnp.where(lane == s, ridges[s], ridge)
    matrix = [
        [
            jnp.broadcast_to(gram[r, s] * scale[r] * scale[s], (traits, TILE)) + (ridge if r == s else 0.0)
            if s <= r
            else None
            for s in range(RIDGES)
        ]
        for r in range(RIDGES)
    ]
    rhs = [jnp.broadcast_to(cross[r] * scale[r], (traits, TILE)) for r in range(RIDGES)]
    weights = small_solve(matrix, rhs)
    parts = []
    for r in range(RIDGES):
        part = raw[r * traits : (r + 1) * traits, :] * scale[r]
        block[r] = part
        parts.append(part)
    for s in range(RIDGES):
        total = weights[0][:, s : s + 1] * parts[0]
        for r in range(1, RIDGES):
            total = total + weights[r][:, s : s + 1] * parts[r]
        stacked[s] = total


def shards(genotypes, phenotypes, folds):
    rows, size = genotypes.shape
    traits = phenotypes.shape[0]
    width = lax.axis_size("ind")
    count = rows * width
    ridges = ridge_list(count)
    per_fold, slots = plan(width)
    own = jnp.concatenate(
        [genotypes.T, phenotypes, jnp.broadcast_to(folds.astype(jnp.bfloat16)[None], (EXTRA, rows))], axis=0
    )
    solved = fit(leave_gram(own, width, size, traits), ridges, width)
    raw, sums = predict(solved, own, width)
    shape = jax.ShapeDtypeStruct((RIDGES, traits, rows), jnp.float32)
    return pl.pallas_call(
        functools.partial(finish_kernel, count, ridges),
        out_shape=(shape, shape),
        compiler_params=pltpu.CompilerParams(vmem_limit_bytes=40 << 20),
    )(sums, raw)


def solution(mesh):
    placed = (P(("cohort", "ind"), None), P(None, ("cohort", "ind")), P(("cohort", "ind")))
    return jax.shard_map(
        shards,
        mesh=mesh,
        in_specs=placed,
        out_specs=(P(None, None, ("cohort", "ind")), P(None, None, ("cohort", "ind"))),
        check_vma=False,
    )
```

```python
import functools

import jax
import jax.numpy as jnp
import numpy as np
from jax import lax
from jax.experimental import pallas as pl
from jax.experimental.pallas import tpu as pltpu
from jax.sharding import PartitionSpec as P

FOLDS = 5
RIDGES = 5
TILE = 128
GROUP = 8
PANEL = 16
EXTRA = 16

heritability = (0.01, 0.25, 0.5, 0.75, 0.99)
epsilon = 1e-06


def ridge_list(count):
    shares = np.asarray(heritability, np.float32)
    return [float(v) for v in np.float32(count) * (np.float32(1.0) - shares) / shares]


def plan(width):
    per_fold = min(width // FOLDS, RIDGES)
    slots = (RIDGES + per_fold - 1) // per_fold
    return per_fold, slots


def eliminate_eight(panel, at, row, lane):
    head = panel[at : at + GROUP]
    columns = [jnp.broadcast_to(head[:, at + j : at + j + 1], (GROUP, TILE)) for j in range(GROUP)]
    inside = (lane >= at) & (lane < at + GROUP)
    reduced = jnp.where(inside, jnp.where(lane - at == row, 1.0, 0.0), head)
    for p in range(GROUP):
        column = columns[p]
        inverse = 1.0 / jnp.broadcast_to(column[p : p + 1], (GROUP, TILE))
        here = row == p

        def eliminate(value):
            pivot = jnp.broadcast_to(value[p : p + 1], (GROUP, TILE))
            return jnp.where(here, pivot * inverse, value - (column * pivot) * inverse)

        reduced = eliminate(reduced)
        for j in range(p + 1, GROUP):
            columns[j] = eliminate(columns[j])
    return reduced


def invert_tiles(tiles):
    lane = lax.broadcasted_iota(jnp.int32, (GROUP, TILE), 1)
    row = lax.broadcasted_iota(jnp.int32, (GROUP, TILE), 0)
    below = lax.broadcasted_iota(jnp.int32, (TILE - PANEL, TILE), 1) < PANEL

    def step(_, tiles):
        results = []
        for tile in tiles:
            panel, rest = tile[:PANEL], tile[PANEL:]
            for at in range(0, PANEL, GROUP):
                reduced = eliminate_eight(panel, at, row, lane)
                pieces = []
                for other in range(0, PANEL, GROUP):
                    if other == at:
                        pieces.append(reduced)
                        continue
                    old = panel[other : other + GROUP]
                    piece = jnp.where((lane >= at) & (lane < at + GROUP), 0.0, old)
                    for j in range(GROUP):
                        piece = piece - jnp.broadcast_to(old[:, at + j : at + j + 1], (GROUP, TILE)) * (
                            jnp.broadcast_to(reduced[j : j + 1], (GROUP, TILE))
                        )
                    pieces.append(piece)
                panel = jnp.concatenate(pieces, axis=0)
            total = jnp.where(below, 0.0, rest) - exact_dot(rest[:, :PANEL], panel)
            results.append(pltpu.roll(jnp.concatenate([total, panel], axis=0), TILE - PANEL, 1))
        return tuple(results)

    return lax.fori_loop(0, TILE // PANEL, step, tuple(tiles))


def exact_dot(a, b):
    return lax.dot_general(
        a, b, (((1,), (0,)), ((), ())), precision=lax.Precision.HIGHEST, preferred_element_type=jnp.float32
    )


def solve_systems(total, work, out, ridges, slots, per_fold, me):
    size = total.shape[0]
    traits = total.shape[1] - size
    eye = lax.broadcasted_iota(jnp.int32, (size, size), 0) == lax.broadcasted_iota(jnp.int32, (size, size), 1)
    for s in range(slots):
        level = lax.rem(lax.rem(me, per_fold) * slots + s, RIDGES)
        ridge = jnp.float32(ridges[0])
        for r in range(1, RIDGES):
            ridge = jnp.where(level == r, jnp.float32(ridges[r]), ridge)
        work[s, :, :size] = total[:, :size] + jnp.where(eye, ridge, 0.0)
        work[s, :, size:] = total[:, size:]
    for first in range(0, size, TILE):
        last = first + TILE
        inverses = invert_tiles([work[s, first:last, first:last] for s in range(slots)])
        for s in range(slots):
            scaled = exact_dot(inverses[s], work[s, first:last, last:])
            if first:
                work[s, :first, last:] = work[s, :first, last:] - exact_dot(work[s, :first, first:last], scaled)
            if last < size:
                work[s, last:, last:] = work[s, last:, last:] - exact_dot(work[s, last:, first:last], scaled)
            work[s, first:last, last:] = scaled
    for s in range(slots):
        out[s * traits : (s + 1) * traits, :] = work[s, :, size:].T.astype(out.dtype)


def layout(width):
    across = 2 if width == 16 else 1
    return width // (2 * across), across


def index_of(z, y, core, across):
    return (z * across + y) * 2 + core


def place_of(me, across):
    return me // (2 * across), lax.rem(me // 2, across), lax.rem(me, 2)


def copy_to(source, target, send, receive, device):
    return pltpu.make_async_remote_copy(
        src_ref=source,
        dst_ref=target,
        send_sem=send,
        recv_sem=receive,
        device_id={"ind": device},
        device_id_type=pl.DeviceIdType.MESH,
    )


def greet(partners):
    barrier = pltpu.get_barrier_semaphore()
    for exists, device in partners:

        @pl.when(exists)
        def _(device=device):
            pl.semaphore_signal(
                barrier, inc=1, device_id={"ind": device}, device_id_type=pl.DeviceIdType.MESH
            )

    expected = jnp.int32(0)
    for exists, _ in partners:
        expected = expected + exists.astype(jnp.int32)
    pl.semaphore_wait(barrier, expected)


UP, DOWN, ACROSS, SIBLING = range(4)


def spread(blocks, send, receive, width, use):
    depth, across = layout(width)
    balanced = across > 1 and depth == 4
    rows = blocks.shape[1]
    cut = -(-rows // 32) * 16
    halves = ((0, cut), (cut, rows - cut))
    me = lax.axis_index("ind")
    z, y, core = place_of(me, across)
    first, last = z == 0, z == depth - 1
    sibling = index_of(z, y, 1 - core, across)
    opposite = index_of(z, lax.rem(y + 1, across), core, across)

    def copy(index, half, way):
        device = {
            UP: index_of(z + 1, y, core, across),
            DOWN: index_of(z - 1, y, core, across),
            ACROSS: opposite,
            SIBLING: sibling,
        }[way]
        piece = blocks.at[index, pl.ds(*halves[half])]
        return copy_to(piece, piece, send.at[way, index, half], receive.at[index, half], device)

    def arrived(index, half):
        copy(index, half, SIBLING).wait_recv()

    def line(step, side):
        origin = z + (2 * side - 1) * step
        valid = (step >= 0) & (origin >= 0) & (origin < depth) & ((step > 0) | (side == 0))
        return origin, valid

    def crossed_line(step, side):
        origin, valid = line(step, side)
        if not balanced:
            return origin, valid
        outer = (first & (side == 0)) | (last & (side == 1))
        late = outer & (step == depth - 1)
        skipped = (first | last) & (step == 1)
        inner = jnp.where(first, 1, depth - 2)
        return jnp.where(late, inner, origin), late | (valid & jnp.logical_not(skipped))

    def crosses(origin, half):
        if not balanced:
            return origin >= 0
        near = (origin == z - 1) | (origin == z + 1)
        ends = (origin == 0) | (origin == depth - 1)
        if half == 1:
            ends = ends | first | last
        return jnp.logical_not(near & ends)

    partner = index_of(z, lax.rem(y + 1, across), core, across)
    inner_ways = ((UP, first), (DOWN, last))
    outer_ways = ((DOWN, z == 1), (UP, z == depth - 2))

    def body(step, carry):
        for side in (0, 1):
            origin, valid = line(step, side)
            index = index_of(origin, y, core, across)

            @pl.when(valid)
            def _(index=index, side=side, origin=origin):
                for half in (0, 1):

                    @pl.when(step > 0)
                    def _():
                        arrived(index, half)

                    @pl.when(jnp.logical_not(last) if side == 0 else jnp.logical_not(first))
                    def _():
                        copy(index, half, UP if side == 0 else DOWN).start()

                    if side == 0:

                        @pl.when((step == 0) & (z > 0))
                        def _():
                            copy(index, half, DOWN).start()

                    if across > 1:

                        @pl.when(crosses(origin, half))
                        def _():
                            copy(index, half, ACROSS).start()

                    copy(index, half, SIBLING).start()

        if across > 1:
            for side in (0, 1):
                origin, valid = crossed_line(step - 1, side)
                index = index_of(origin, 1 - y, core, across)

                @pl.when(valid)
                def _(index=index):
                    for half in (0, 1):
                        arrived(index, half)
                        copy(index, half, SIBLING).start()

        if balanced:
            for way, here in inner_ways:

                @pl.when((step == 1) & here)
                def _(way=way):
                    for half in (0, 1):
                        copy(partner, half, way).start()

            for way, here in outer_ways:

                @pl.when((step == 2) & here)
                def _(way=way):
                    copy(partner, 1, way).start()

        def visit(turn, inner):
            side = lax.rem(turn, 2)
            crossed = lax.rem(turn // 2, across)
            shared = turn // (2 * across)
            when = step - crossed - shared
            origin, valid = line(when, side)
            if across > 1:
                other_origin, other_valid = crossed_line(when, side)
                origin = jnp.where(crossed == 1, other_origin, origin)
                valid = ((crossed == 1) & other_valid) | ((crossed == 0) & valid)
            index = index_of(origin, lax.rem(y + crossed, across), lax.rem(core + shared, 2), across)

            @pl.when(valid)
            def _():
                @pl.when(shared == 1)
                def _():
                    arrived(index, 0)
                    arrived(index, 1)

                use(index)

            return inner

        return lax.fori_loop(0, 4 * across, visit, carry)

    lax.fori_loop(0, depth + across, body, 0)

    def settle(origin, carry):
        own = index_of(origin, y, core, across)
        for half in (0, 1):

            @pl.when((z < depth - 1) & (origin <= z))
            def _():
                copy(own, half, UP).wait_send()

            @pl.when((z > 0) & (origin >= z))
            def _():
                copy(own, half, DOWN).wait_send()

            copy(own, half, SIBLING).wait_send()
            if across > 1:

                @pl.when(crosses(origin, half))
                def _():
                    copy(own, half, ACROSS).wait_send()

                copy(index_of(origin, 1 - y, core, across), half, SIBLING).wait_send()
        return carry

    lax.fori_loop(0, depth, settle, 0)
    if balanced:
        for way, here in inner_ways:

            @pl.when(here)
            def _(way=way):
                for half in (0, 1):
                    copy(partner, half, way).wait_send()

        for way, here in outer_ways:

            @pl.when(here)
            def _(way=way):
                copy(partner, 1, way).wait_send()


def spread_partners(width):
    depth, across = layout(width)
    me = lax.axis_index("ind")
    z, y, core = place_of(me, across)
    partners = [
        (z < depth - 1, index_of(z + 1, y, core, across)),
        (z > 0, index_of(z - 1, y, core, across)),
        (z >= 0, index_of(z, y, 1 - core, across)),
    ]
    if across > 1:
        partners.append((z >= 0, index_of(z, 1 - y, core, across)))
    return partners


def gram_kernel(width, per_fold, own, total, blocks, send, receive, local):
    me = lax.axis_index("ind")
    rows, size = total.shape[1], total.shape[0]
    fold = jnp.minimum(me // per_fold, FOLDS - 1).astype(jnp.float32)
    fill = pltpu.make_async_copy(own, blocks.at[me], local)
    fill.start()
    greet(spread_partners(width))
    total[...] = jnp.zeros_like(total)
    fill.wait()

    def use(index):
        keep = (blocks[index, rows : rows + EXTRA, :].astype(jnp.float32)[:1] != fold).astype(jnp.bfloat16)
        total[...] += lax.dot_general(
            blocks[index, :size, :] * keep,
            blocks[index, :rows, :],
            (((1,), (1,)), ((), ())),
            preferred_element_type=jnp.float32,
        )

    spread(blocks, send, receive, width, use)


def leave_gram(own, width, size, traits):
    rows, individuals = own.shape
    per_fold, _ = plan(width)
    return pl.pallas_call(
        functools.partial(gram_kernel, width, per_fold),
        out_shape=jax.ShapeDtypeStruct((size, size + traits), jnp.float32),
        in_specs=[pl.BlockSpec(memory_space=pl.ANY)],
        out_specs=pl.BlockSpec(memory_space=pltpu.VMEM),
        scratch_shapes=[
            pltpu.VMEM((width, rows, individuals), jnp.bfloat16),
            pltpu.SemaphoreType.DMA((4, width, 2)),
            pltpu.SemaphoreType.DMA((width, 2)),
            pltpu.SemaphoreType.DMA,
        ],
        compiler_params=pltpu.CompilerParams(
            collective_id=0,
            has_side_effects=True,
            vmem_limit_bytes=(12 << 20) + 2 * width * rows * individuals,
        ),
    )(own)


def fit_kernel(ridges, per_fold, slots, total, out, work):
    solve_systems(total, work, out, ridges, slots, per_fold, lax.axis_index("ind"))


def fit(total, ridges, width):
    per_fold, slots = plan(width)
    size = total.shape[0]
    traits = total.shape[1] - size
    return pl.pallas_call(
        functools.partial(fit_kernel, ridges, per_fold, slots),
        out_shape=jax.ShapeDtypeStruct((slots * traits, size), jnp.bfloat16),
        scratch_shapes=[pltpu.VMEM((slots, size, size + traits), jnp.float32)],
        compiler_params=pltpu.CompilerParams(vmem_limit_bytes=40 << 20),
    )(total)


def small_solve(matrix, rhs):
    size = len(rhs)
    lower = {}
    for column in range(size):
        total = matrix[column][column]
        for inner in range(column):
            total = total - lower[column, inner] * lower[column, inner]
        lower[column, column] = jnp.sqrt(total)
        for row in range(column + 1, size):
            total = matrix[row][column]
            for inner in range(column):
                total = total - lower[row, inner] * lower[column, inner]
            lower[row, column] = total / lower[column, column]
    forward = []
    for row in range(size):
        total = rhs[row]
        for inner in range(row):
            total = total - lower[row, inner] * forward[inner]
        forward.append(total / lower[row, row])
    backward = {}
    for row in reversed(range(size)):
        total = forward[row]
        for inner in range(row + 1, size):
            total = total - lower[inner, row] * backward[inner]
        backward[row] = total / lower[row, row]
    return [backward[row] for row in range(size)]


def predict_kernel(
    width, per_fold, slots, solved, block, raw, sums,
    coefficients, near, far, send, receive, near_send, near_receive, far_send, far_receive,
):
    size = coefficients.shape[2]
    traits = coefficients.shape[1] // slots
    rows = size + traits
    depth, across = layout(width)
    me = lax.axis_index("ind")
    z, y, core = place_of(me, across)
    corner = y * 2 + core
    near_devices = [(lax.rem(corner + k, 2 * across), k) for k in range(1, 2 * across)]
    far_devices = [(lax.rem(z + k, depth), k) for k in range(1, depth)]
    always = me >= 0
    coefficients[me] = solved[...]
    greet(
        [(always, z * 2 * across + other) for other, _ in near_devices]
        + [(always, other * 2 * across + corner) for other, _ in far_devices]
    )
    spread(coefficients, send, receive, width, lambda index: None)
    geno = block[:size, :]
    phen = block[size:rows, :].astype(jnp.float32)
    folds = block[rows : rows + 1, :].astype(jnp.float32)
    total = None
    for fold in range(FOLDS):
        masked = geno * (folds == float(fold)).astype(jnp.bfloat16)
        flat = jnp.concatenate(
            [
                coefficients[fold * per_fold + r // slots, pl.ds(r % slots * traits, traits)]
                for r in range(RIDGES)
            ],
            axis=0,
        )
        part = lax.dot_general(flat, masked, (((1,), (0,)), ((), ())), preferred_element_type=jnp.float32)
        total = part if total is None else total + part
    raw[...] = total
    parts = [total[r * traits : (r + 1) * traits] for r in range(RIDGES)]
    lane = lax.broadcasted_iota(jnp.int32, (traits, TILE), 1)
    packed = jnp.zeros((traits, TILE), jnp.float32)
    place = 0
    for r in range(RIDGES):
        for other in parts[: r + 1] + [phen]:
            packed = jnp.where(lane == place, jnp.sum(parts[r] * other, axis=1, keepdims=True), packed)
            place += 1

    def exchange(buffer, mine, devices, sends, receives, device_of):
        copies = []
        for other, k in devices:
            copy = copy_to(
                buffer.at[mine], buffer.at[mine], sends.at[k], receives.at[mine], device_of(other)
            )
            copy.start()
            copies.append(copy)
        for other, k in devices:
            copy_to(
                buffer.at[other], buffer.at[other], sends.at[k], receives.at[other], device_of(other)
            ).wait_recv()
        for copy in copies:
            copy.wait_send()

    near[corner] = packed
    exchange(near, corner, near_devices, near_send, near_receive, lambda other: z * 2 * across + other)
    far[z] = jnp.sum(near[...], axis=0)
    exchange(far, z, far_devices, far_send, far_receive, lambda other: other * 2 * across + corner)
    sums[...] = jnp.sum(far[...], axis=0)


def predict(solved, own, width):
    size = solved.shape[1]
    per_fold, slots = plan(width)
    traits = solved.shape[0] // slots
    depth, across = layout(width)
    return pl.pallas_call(
        functools.partial(predict_kernel, width, per_fold, slots),
        out_shape=(
            jax.ShapeDtypeStruct((RIDGES * traits, own.shape[1]), jnp.float32),
            jax.ShapeDtypeStruct((traits, TILE), jnp.float32),
        ),
        scratch_shapes=[
            pltpu.VMEM((width, slots * traits, size), jnp.bfloat16),
            pltpu.VMEM((2 * across, traits, TILE), jnp.float32),
            pltpu.VMEM((depth, traits, TILE), jnp.float32),
            pltpu.SemaphoreType.DMA((4, width, 2)),
            pltpu.SemaphoreType.DMA((width, 2)),
            pltpu.SemaphoreType.DMA((2 * across,)),
            pltpu.SemaphoreType.DMA((2 * across,)),
            pltpu.SemaphoreType.DMA((depth,)),
            pltpu.SemaphoreType.DMA((depth,)),
        ],
        compiler_params=pltpu.CompilerParams(
            collective_id=1, has_side_effects=True, vmem_limit_bytes=40 << 20
        ),
    )(solved, own)


def finish_kernel(count, ridges, sums, raw, block, stacked):
    traits = sums.shape[0]
    gram = {}
    cross = []
    place = 0
    for r in range(RIDGES):
        for s in range(r + 1):
            gram[r, s] = sums[:, place : place + 1]
            place += 1
        cross.append(sums[:, place : place + 1])
        place += 1
    scale = [1.0 / jnp.sqrt(gram[r, r] / count + epsilon) for r in range(RIDGES)]
    lane = lax.broadcasted_iota(jnp.int32, (traits, TILE), 1)
    ridge = jnp.full((traits, TILE), ridges[0], jnp.float32)
    for s in range(1, RIDGES):
        ridge = jnp.where(lane == s, ridges[s], ridge)
    matrix = [
        [
            jnp.broadcast_to(gram[r, s] * scale[r] * scale[s], (traits, TILE)) + (ridge if r == s else 0.0)
            if s <= r
            else None
            for s in range(RIDGES)
        ]
        for r in range(RIDGES)
    ]
    rhs = [jnp.broadcast_to(cross[r] * scale[r], (traits, TILE)) for r in range(RIDGES)]
    weights = small_solve(matrix, rhs)
    parts = []
    for r in range(RIDGES):
        part = raw[r * traits : (r + 1) * traits, :] * scale[r]
        block[r] = part
        parts.append(part)
    for s in range(RIDGES):
        total = weights[0][:, s : s + 1] * parts[0]
        for r in range(1, RIDGES):
            total = total + weights[r][:, s : s + 1] * parts[r]
        stacked[s] = total


def shards(genotypes, phenotypes, folds):
    rows, size = genotypes.shape
    traits = phenotypes.shape[0]
    width = lax.axis_size("ind")
    count = rows * width
    ridges = ridge_list(count)
    per_fold, slots = plan(width)
    own = jnp.concatenate(
        [genotypes.T, phenotypes, jnp.broadcast_to(folds.astype(jnp.bfloat16)[None], (EXTRA, rows))], axis=0
    )
    solved = fit(leave_gram(own, width, size, traits), ridges, width)
    raw, sums = predict(solved, own, width)
    shape = jax.ShapeDtypeStruct((RIDGES, traits, rows), jnp.float32)
    return pl.pallas_call(
        functools.partial(finish_kernel, count, ridges),
        out_shape=(shape, shape),
        compiler_params=pltpu.CompilerParams(vmem_limit_bytes=40 << 20),
    )(sums, raw)


def solution(mesh):
    placed = (P(("cohort", "ind"), None), P(None, ("cohort", "ind")), P(("cohort", "ind")))
    return jax.shard_map(
        shards,
        mesh=mesh,
        in_specs=placed,
        out_specs=(P(None, None, ("cohort", "ind")), P(None, None, ("cohort", "ind"))),
        check_vma=False,
    )
```

```python
import functools

import jax
import jax.numpy as jnp
import numpy as np
from jax import lax
from jax.experimental import pallas as pl
from jax.experimental.pallas import tpu as pltpu
from jax.sharding import PartitionSpec as P

FOLDS = 5
RIDGES = 5
TILE = 128
GROUP = 8
PANEL = 16
SUMS = 24
EXTRA = 16

heritability = (0.01, 0.25, 0.5, 0.75, 0.99)
epsilon = 1e-06


def ridge_list(count):
    shares = np.asarray(heritability, np.float32)
    return [float(v) for v in np.float32(count) * (np.float32(1.0) - shares) / shares]


def plan(width):
    per_fold = min(width // FOLDS, RIDGES)
    slots = (RIDGES + per_fold - 1) // per_fold
    return per_fold, slots


def eliminate_eight(panel, at, row, lane):
    head = panel[at : at + GROUP]
    columns = [jnp.broadcast_to(head[:, at + j : at + j + 1], (GROUP, TILE)) for j in range(GROUP)]
    inside = (lane >= at) & (lane < at + GROUP)
    reduced = jnp.where(inside, jnp.where(lane - at == row, 1.0, 0.0), head)
    for p in range(GROUP):
        column = columns[p]
        inverse = 1.0 / jnp.broadcast_to(column[p : p + 1], (GROUP, TILE))
        here = row == p

        def eliminate(value):
            pivot = jnp.broadcast_to(value[p : p + 1], (GROUP, TILE))
            return jnp.where(here, pivot * inverse, value - (column * pivot) * inverse)

        reduced = eliminate(reduced)
        for j in range(p + 1, GROUP):
            columns[j] = eliminate(columns[j])
    return reduced


def invert_tiles(tiles):
    lane = lax.broadcasted_iota(jnp.int32, (GROUP, TILE), 1)
    row = lax.broadcasted_iota(jnp.int32, (GROUP, TILE), 0)
    below = lax.broadcasted_iota(jnp.int32, (TILE - PANEL, TILE), 1) < PANEL

    def step(_, tiles):
        results = []
        for tile in tiles:
            panel, rest = tile[:PANEL], tile[PANEL:]
            for at in range(0, PANEL, GROUP):
                reduced = eliminate_eight(panel, at, row, lane)
                pieces = []
                for other in range(0, PANEL, GROUP):
                    if other == at:
                        pieces.append(reduced)
                        continue
                    old = panel[other : other + GROUP]
                    piece = jnp.where((lane >= at) & (lane < at + GROUP), 0.0, old)
                    for j in range(GROUP):
                        piece = piece - jnp.broadcast_to(old[:, at + j : at + j + 1], (GROUP, TILE)) * (
                            jnp.broadcast_to(reduced[j : j + 1], (GROUP, TILE))
                        )
                    pieces.append(piece)
                panel = jnp.concatenate(pieces, axis=0)
            total = jnp.where(below, 0.0, rest) - exact_dot(rest[:, :PANEL], panel)
            results.append(pltpu.roll(jnp.concatenate([total, panel], axis=0), TILE - PANEL, 1))
        return tuple(results)

    return lax.fori_loop(0, TILE // PANEL, step, tuple(tiles))


def exact_dot(a, b):
    return lax.dot_general(
        a, b, (((1,), (0,)), ((), ())), precision=lax.Precision.HIGHEST, preferred_element_type=jnp.float32
    )


def solve_systems(total, work, out, ridges, slots, per_fold, me):
    size = total.shape[0]
    traits = total.shape[1] - size
    eye = lax.broadcasted_iota(jnp.int32, (size, size), 0) == lax.broadcasted_iota(jnp.int32, (size, size), 1)
    for s in range(slots):
        level = lax.rem(lax.rem(me, per_fold) * slots + s, RIDGES)
        ridge = jnp.float32(ridges[0])
        for r in range(1, RIDGES):
            ridge = jnp.where(level == r, jnp.float32(ridges[r]), ridge)
        work[s, :, :size] = total[:, :size] + jnp.where(eye, ridge, 0.0)
        work[s, :, size:] = total[:, size:]
    for first in range(0, size, TILE):
        last = first + TILE
        inverses = invert_tiles([work[s, first:last, first:last] for s in range(slots)])
        for s in range(slots):
            scaled = exact_dot(inverses[s], work[s, first:last, last:])
            if first:
                work[s, :first, last:] = work[s, :first, last:] - exact_dot(work[s, :first, first:last], scaled)
            if last < size:
                work[s, last:, last:] = work[s, last:, last:] - exact_dot(work[s, last:, first:last], scaled)
            work[s, first:last, last:] = scaled
    for s in range(slots):
        out[s * traits : (s + 1) * traits, :] = work[s, :, size:].T.astype(out.dtype)


def layout(width):
    across = 2 if width == 16 else 1
    return width // (2 * across), across


def index_of(z, y, core, across):
    return (z * across + y) * 2 + core


def place_of(me, across):
    return me // (2 * across), lax.rem(me // 2, across), lax.rem(me, 2)


def copy_to(source, target, send, receive, device):
    return pltpu.make_async_remote_copy(
        src_ref=source,
        dst_ref=target,
        send_sem=send,
        recv_sem=receive,
        device_id={"ind": device},
        device_id_type=pl.DeviceIdType.MESH,
    )


def greet(partners, meanwhile):
    barrier = pltpu.get_barrier_semaphore()
    for exists, device in partners:

        @pl.when(exists)
        def _(device=device):
            pl.semaphore_signal(
                barrier, inc=1, device_id={"ind": device}, device_id_type=pl.DeviceIdType.MESH
            )

    meanwhile()
    expected = jnp.int32(0)
    for exists, _ in partners:
        expected = expected + exists.astype(jnp.int32)
    pl.semaphore_wait(barrier, expected)


UP, DOWN, ACROSS, SIBLING = range(4)


def spread(blocks, send, receive, width, use, needed):
    depth, across = layout(width)
    balanced = across > 1 and depth == 4
    rows = blocks.shape[1]
    cut = -(-rows // 32) * 16
    halves = ((0, cut), (cut, rows - cut))
    me = lax.axis_index("ind")
    z, y, core = place_of(me, across)
    first, last = z == 0, z == depth - 1
    sibling = index_of(z, y, 1 - core, across)
    opposite = index_of(z, lax.rem(y + 1, across), core, across)

    def copy(index, half, way):
        device = {
            UP: index_of(z + 1, y, core, across),
            DOWN: index_of(z - 1, y, core, across),
            ACROSS: opposite,
            SIBLING: sibling,
        }[way]
        piece = blocks.at[index, pl.ds(*halves[half])]
        return copy_to(piece, piece, send.at[way, index, half], receive.at[index, half], device)

    def arrived(index, half):
        copy(index, half, SIBLING).wait_recv()

    def line(step, side):
        origin = z + (2 * side - 1) * step
        valid = (step >= 0) & (origin >= 0) & (origin < depth) & ((step > 0) | (side == 0))
        return origin, valid

    def crossed_line(step, side):
        origin, valid = line(step, side)
        if not balanced:
            return origin, valid
        outer = (first & (side == 0)) | (last & (side == 1))
        late = outer & (step == depth - 1)
        skipped = (first | last) & (step == 1)
        inner = jnp.where(first, 1, depth - 2)
        return jnp.where(late, inner, origin), late | (valid & jnp.logical_not(skipped))

    def crosses(origin, half):
        if not balanced:
            return origin >= 0
        near = (origin == z - 1) | (origin == z + 1)
        ends = (origin == 0) | (origin == depth - 1)
        if half == 1:
            ends = ends | first | last
        return jnp.logical_not(near & ends)

    partner = index_of(z, lax.rem(y + 1, across), core, across)
    inner_ways = ((UP, first), (DOWN, last))
    outer_ways = ((DOWN, z == 1), (UP, z == depth - 2))

    def body(step, carry):
        for side in (0, 1):
            origin, valid = line(step, side)
            index = index_of(origin, y, core, across)

            @pl.when(valid)
            def _(index=index, side=side, origin=origin):
                for half in (0, 1):

                    @pl.when(needed(index, half))
                    def _(half=half):
                        @pl.when(step > 0)
                        def _():
                            arrived(index, half)

                        @pl.when(jnp.logical_not(last) if side == 0 else jnp.logical_not(first))
                        def _():
                            copy(index, half, UP if side == 0 else DOWN).start()

                        if side == 0:

                            @pl.when((step == 0) & (z > 0))
                            def _():
                                copy(index, half, DOWN).start()

                        if across > 1:

                            @pl.when(crosses(origin, half))
                            def _():
                                copy(index, half, ACROSS).start()

                        copy(index, half, SIBLING).start()

        if across > 1:
            for side in (0, 1):
                origin, valid = crossed_line(step - 1, side)
                index = index_of(origin, 1 - y, core, across)

                @pl.when(valid)
                def _(index=index):
                    for half in (0, 1):

                        @pl.when(needed(index, half))
                        def _(half=half):
                            arrived(index, half)
                            copy(index, half, SIBLING).start()

        if balanced:
            for way, here in inner_ways:

                for half in (0, 1):

                    @pl.when((step == 1) & here & needed(partner, half))
                    def _(way=way, half=half):
                        copy(partner, half, way).start()

            for way, here in outer_ways:

                @pl.when((step == 2) & here & needed(partner, 1))
                def _(way=way):
                    copy(partner, 1, way).start()

        def visit(turn, inner):
            side = lax.rem(turn, 2)
            crossed = lax.rem(turn // 2, across)
            shared = turn // (2 * across)
            when = step - crossed - shared
            origin, valid = line(when, side)
            if across > 1:
                other_origin, other_valid = crossed_line(when, side)
                origin = jnp.where(crossed == 1, other_origin, origin)
                valid = ((crossed == 1) & other_valid) | ((crossed == 0) & valid)
            index = index_of(origin, lax.rem(y + crossed, across), lax.rem(core + shared, 2), across)

            @pl.when(valid)
            def _():
                for half in (0, 1):

                    @pl.when((shared == 1) & needed(index, half))
                    def _(half=half):
                        arrived(index, half)

                use(index)

            return inner

        return lax.fori_loop(0, 4 * across, visit, carry)

    lax.fori_loop(0, depth + across, body, 0)

    def settle(origin, carry):
        own = index_of(origin, y, core, across)
        for half in (0, 1):

            wanted = needed(own, half)

            @pl.when(wanted & (z < depth - 1) & (origin <= z))
            def _():
                copy(own, half, UP).wait_send()

            @pl.when(wanted & (z > 0) & (origin >= z))
            def _():
                copy(own, half, DOWN).wait_send()

            @pl.when(wanted)
            def _():
                copy(own, half, SIBLING).wait_send()

            if across > 1:

                @pl.when(wanted & crosses(origin, half))
                def _():
                    copy(own, half, ACROSS).wait_send()

                other = index_of(origin, 1 - y, core, across)

                @pl.when(needed(other, half))
                def _():
                    copy(other, half, SIBLING).wait_send()
        return carry

    lax.fori_loop(0, depth, settle, 0)
    if balanced:
        for way, here in inner_ways:

            for half in (0, 1):

                @pl.when(here & needed(partner, half))
                def _(way=way, half=half):
                    copy(partner, half, way).wait_send()

        for way, here in outer_ways:

            @pl.when(here & needed(partner, 1))
            def _(way=way):
                copy(partner, 1, way).wait_send()


def spread_partners(width):
    depth, across = layout(width)
    me = lax.axis_index("ind")
    z, y, core = place_of(me, across)
    partners = [
        (z < depth - 1, index_of(z + 1, y, core, across)),
        (z > 0, index_of(z - 1, y, core, across)),
        (z >= 0, index_of(z, y, 1 - core, across)),
    ]
    if across > 1:
        partners.append((z >= 0, index_of(z, 1 - y, core, across)))
    return partners


def gram_kernel(width, per_fold, genotypes, phenotypes, folds, total, own, blocks, send, receive):
    me = lax.axis_index("ind")
    rows, size = total.shape[1], total.shape[0]
    fold = jnp.minimum(me // per_fold, FOLDS - 1).astype(jnp.float32)

    def prepare():
        members = folds[...].astype(jnp.float32)
        block = jnp.concatenate(
            [
                genotypes[...].T,
                phenotypes[...],
                jnp.broadcast_to(members, (EXTRA, members.shape[1])).astype(jnp.bfloat16),
            ],
            axis=0,
        )
        blocks[me] = block
        own[...] = block
        total[...] = jnp.zeros_like(total)

    greet(spread_partners(width), prepare)

    def use(index):
        keep = (blocks[index, rows : rows + EXTRA, :].astype(jnp.float32)[:1] != fold).astype(jnp.bfloat16)
        total[...] += lax.dot_general(
            blocks[index, :size, :] * keep,
            blocks[index, :rows, :],
            (((1,), (1,)), ((), ())),
            preferred_element_type=jnp.float32,
        )

    spread(blocks, send, receive, width, use, lambda index, half: index >= 0)


def leave_gram(genotypes, phenotypes, folds, width):
    individuals, size = genotypes.shape
    traits = phenotypes.shape[0]
    rows = size + traits + EXTRA
    per_fold, _ = plan(width)
    return pl.pallas_call(
        functools.partial(gram_kernel, width, per_fold),
        out_shape=(
            jax.ShapeDtypeStruct((size, size + traits), jnp.float32),
            jax.ShapeDtypeStruct((rows, individuals), jnp.bfloat16),
        ),
        scratch_shapes=[
            pltpu.VMEM((width, rows, individuals), jnp.bfloat16),
            pltpu.SemaphoreType.DMA((4, width, 2)),
            pltpu.SemaphoreType.DMA((width, 2)),
        ],
        compiler_params=pltpu.CompilerParams(
            collective_id=0,
            has_side_effects=True,
            vmem_limit_bytes=(14 << 20) + 2 * width * rows * individuals,
        ),
    )(genotypes, phenotypes, folds[None])


def fit_kernel(ridges, per_fold, slots, total, out, work):
    solve_systems(total, work, out, ridges, slots, per_fold, lax.axis_index("ind"))


def fit(total, ridges, width):
    per_fold, slots = plan(width)
    size = total.shape[0]
    traits = total.shape[1] - size
    return pl.pallas_call(
        functools.partial(fit_kernel, ridges, per_fold, slots),
        out_shape=jax.ShapeDtypeStruct((slots * traits, size), jnp.bfloat16),
        scratch_shapes=[pltpu.VMEM((slots, size, size + traits), jnp.float32)],
        compiler_params=pltpu.CompilerParams(vmem_limit_bytes=40 << 20),
    )(total)


def small_solve(matrix, rhs):
    size = len(rhs)
    lower = {}
    for column in range(size):
        total = matrix[column][column]
        for inner in range(column):
            total = total - lower[column, inner] * lower[column, inner]
        lower[column, column] = jnp.sqrt(total)
        for row in range(column + 1, size):
            total = matrix[row][column]
            for inner in range(column):
                total = total - lower[row, inner] * lower[column, inner]
            lower[row, column] = total / lower[column, column]
    forward = []
    for row in range(size):
        total = rhs[row]
        for inner in range(row):
            total = total - lower[row, inner] * forward[inner]
        forward.append(total / lower[row, row])
    backward = {}
    for row in reversed(range(size)):
        total = forward[row]
        for inner in range(row + 1, size):
            total = total - lower[inner, row] * backward[inner]
        backward[row] = total / lower[row, row]
    return [backward[row] for row in range(size)]


def predict_kernel(
    width, per_fold, slots, solved, block, raw, sums,
    coefficients, near, far, send, receive, near_send, near_receive, far_send, far_receive,
):
    size = coefficients.shape[2]
    traits = coefficients.shape[1] // slots
    rows = size + traits
    depth, across = layout(width)
    me = lax.axis_index("ind")
    z, y, core = place_of(me, across)
    corner = y * 2 + core
    near_devices = [(lax.rem(corner + k, 2 * across), k) for k in range(1, 2 * across)]
    far_devices = [(lax.rem(z + k, depth), k) for k in range(1, depth)]
    always = me >= 0
    geno = block[:size, :]
    phen = block[size:rows, :].astype(jnp.float32)
    folds = block[rows : rows + 1, :].astype(jnp.float32)

    def prepare():
        coefficients[me] = solved[...]
        raw[...] = jnp.zeros_like(raw)

    greet(
        [(always, z * 2 * across + other) for other, _ in near_devices]
        + [(always, other * 2 * across + corner) for other, _ in far_devices],
        prepare,
    )
    cut = -(-slots * traits // 32) * 16

    def level_of(index, slot):
        return lax.rem(index, per_fold) * slots + slot

    def needed(index, half):
        return (index < FOLDS * per_fold) & (level_of(index, half * cut // traits) < RIDGES)

    def use(index):
        fold = index // per_fold
        masked = geno * (folds == fold.astype(jnp.float32)).astype(jnp.bfloat16)
        for slot in range(slots):
            level = level_of(index, slot)

            @pl.when((fold < FOLDS) & (level < RIDGES))
            def _(slot=slot, level=level):
                flat = coefficients[index, slot * traits : (slot + 1) * traits, :]
                raw[pl.ds(pl.multiple_of(level * traits, traits), traits), :] += lax.dot_general(
                    flat, masked, (((1,), (0,)), ((), ())), preferred_element_type=jnp.float32
                )

    spread(coefficients, send, receive, width, use, needed)
    total = raw[...]
    parts = [total[r * traits : (r + 1) * traits] for r in range(RIDGES)]
    lane = lax.broadcasted_iota(jnp.int32, (traits, TILE), 1)
    packed = jnp.zeros((traits, TILE), jnp.float32)
    place = 0
    for r in range(RIDGES):
        for other in parts[: r + 1] + [phen]:
            packed = jnp.where(lane == place, jnp.sum(parts[r] * other, axis=1, keepdims=True), packed)
            place += 1

    def exchange(buffer, mine, devices, sends, receives, device_of):
        copies = []
        for other, k in devices:
            copy = copy_to(
                buffer.at[mine], buffer.at[mine], sends.at[k], receives.at[mine], device_of(other)
            )
            copy.start()
            copies.append(copy)
        for other, k in devices:
            copy_to(
                buffer.at[other], buffer.at[other], sends.at[k], receives.at[other], device_of(other)
            ).wait_recv()
        for copy in copies:
            copy.wait_send()

    spare = jnp.zeros((SUMS, TILE - traits), jnp.float32)
    near[corner] = jnp.concatenate([packed.T[:SUMS], spare], axis=1)
    exchange(near, corner, near_devices, near_send, near_receive, lambda other: z * 2 * across + other)
    far[z] = jnp.sum(near[...], axis=0)
    exchange(far, z, far_devices, far_send, far_receive, lambda other: other * 2 * across + corner)
    gathered = jnp.sum(far[...], axis=0)
    filled = jnp.concatenate([gathered, jnp.zeros((TILE - SUMS, TILE), jnp.float32)], axis=0)
    sums[...] = filled.T[:traits]


def predict(solved, own, width):
    size = solved.shape[1]
    per_fold, slots = plan(width)
    traits = solved.shape[0] // slots
    depth, across = layout(width)
    return pl.pallas_call(
        functools.partial(predict_kernel, width, per_fold, slots),
        out_shape=(
            jax.ShapeDtypeStruct((RIDGES * traits, own.shape[1]), jnp.float32),
            jax.ShapeDtypeStruct((traits, TILE), jnp.float32),
        ),
        scratch_shapes=[
            pltpu.VMEM((width, slots * traits, size), jnp.bfloat16),
            pltpu.VMEM((2 * across, SUMS, TILE), jnp.float32),
            pltpu.VMEM((depth, SUMS, TILE), jnp.float32),
            pltpu.SemaphoreType.DMA((4, width, 2)),
            pltpu.SemaphoreType.DMA((width, 2)),
            pltpu.SemaphoreType.DMA((2 * across,)),
            pltpu.SemaphoreType.DMA((2 * across,)),
            pltpu.SemaphoreType.DMA((depth,)),
            pltpu.SemaphoreType.DMA((depth,)),
        ],
        compiler_params=pltpu.CompilerParams(
            collective_id=1, has_side_effects=True, vmem_limit_bytes=40 << 20
        ),
    )(solved, own)


def finish_kernel(count, ridges, sums, raw, block, stacked):
    traits = sums.shape[0]
    gram = {}
    cross = []
    place = 0
    for r in range(RIDGES):
        for s in range(r + 1):
            gram[r, s] = sums[:, place : place + 1]
            place += 1
        cross.append(sums[:, place : place + 1])
        place += 1
    scale = [1.0 / jnp.sqrt(gram[r, r] / count + epsilon) for r in range(RIDGES)]
    lane = lax.broadcasted_iota(jnp.int32, (traits, TILE), 1)
    ridge = jnp.full((traits, TILE), ridges[0], jnp.float32)
    for s in range(1, RIDGES):
        ridge = jnp.where(lane == s, ridges[s], ridge)
    matrix = [
        [
            jnp.broadcast_to(gram[r, s] * scale[r] * scale[s], (traits, TILE)) + (ridge if r == s else 0.0)
            if s <= r
            else None
            for s in range(RIDGES)
        ]
        for r in range(RIDGES)
    ]
    rhs = [jnp.broadcast_to(cross[r] * scale[r], (traits, TILE)) for r in range(RIDGES)]
    weights = small_solve(matrix, rhs)
    parts = []
    for r in range(RIDGES):
        part = raw[r * traits : (r + 1) * traits, :] * scale[r]
        block[r] = part
        parts.append(part)
    for s in range(RIDGES):
        total = weights[0][:, s : s + 1] * parts[0]
        for r in range(1, RIDGES):
            total = total + weights[r][:, s : s + 1] * parts[r]
        stacked[s] = total


def shards(genotypes, phenotypes, folds):
    rows = genotypes.shape[0]
    traits = phenotypes.shape[0]
    width = lax.axis_size("ind")
    count = rows * width
    ridges = ridge_list(count)
    total, own = leave_gram(genotypes, phenotypes, folds, width)
    solved = fit(total, ridges, width)
    raw, sums = predict(solved, own, width)
    shape = jax.ShapeDtypeStruct((RIDGES, traits, rows), jnp.float32)
    return pl.pallas_call(
        functools.partial(finish_kernel, count, ridges),
        out_shape=(shape, shape),
        compiler_params=pltpu.CompilerParams(vmem_limit_bytes=40 << 20),
    )(sums, raw)


def solution(mesh):
    placed = (P(("cohort", "ind"), None), P(None, ("cohort", "ind")), P(("cohort", "ind")))
    return jax.shard_map(
        shards,
        mesh=mesh,
        in_specs=placed,
        out_specs=(P(None, None, ("cohort", "ind")), P(None, None, ("cohort", "ind"))),
        check_vma=False,
    )
```

```python
import functools

import jax
import jax.numpy as jnp
import numpy as np
from jax import lax
from jax.experimental import pallas as pl
from jax.experimental.pallas import tpu as pltpu
from jax.sharding import PartitionSpec as P

FOLDS = 5
RIDGES = 5
TILE = 128
GROUP = 8
PANEL = 16
SUMS = 24
EXTRA = 16

heritability = (0.01, 0.25, 0.5, 0.75, 0.99)
epsilon = 1e-06


def ridge_list(count):
    shares = np.asarray(heritability, np.float32)
    return [float(v) for v in np.float32(count) * (np.float32(1.0) - shares) / shares]


def plan(width):
    per_fold = min(width // FOLDS, RIDGES)
    slots = (RIDGES + per_fold - 1) // per_fold
    return per_fold, slots


def eliminate_eight(panel, at, row, lane):
    head = panel[at : at + GROUP]
    columns = [jnp.broadcast_to(head[:, at + j : at + j + 1], (GROUP, TILE)) for j in range(GROUP)]
    inside = (lane >= at) & (lane < at + GROUP)
    reduced = jnp.where(inside, jnp.where(lane - at == row, 1.0, 0.0), head)
    for p in range(GROUP):
        column = columns[p]
        inverse = 1.0 / jnp.broadcast_to(column[p : p + 1], (GROUP, TILE))
        here = row == p

        def eliminate(value):
            pivot = jnp.broadcast_to(value[p : p + 1], (GROUP, TILE))
            return jnp.where(here, pivot * inverse, value - (column * pivot) * inverse)

        reduced = eliminate(reduced)
        for j in range(p + 1, GROUP):
            columns[j] = eliminate(columns[j])
    return reduced


def invert_tiles(tiles):
    lane = lax.broadcasted_iota(jnp.int32, (GROUP, TILE), 1)
    row = lax.broadcasted_iota(jnp.int32, (GROUP, TILE), 0)
    below = lax.broadcasted_iota(jnp.int32, (TILE - PANEL, TILE), 1) < PANEL

    def step(_, tiles):
        results = []
        for tile in tiles:
            panel, rest = tile[:PANEL], tile[PANEL:]
            for at in range(0, PANEL, GROUP):
                reduced = eliminate_eight(panel, at, row, lane)
                pieces = []
                for other in range(0, PANEL, GROUP):
                    if other == at:
                        pieces.append(reduced)
                        continue
                    old = panel[other : other + GROUP]
                    piece = jnp.where((lane >= at) & (lane < at + GROUP), 0.0, old)
                    for j in range(GROUP):
                        piece = piece - jnp.broadcast_to(old[:, at + j : at + j + 1], (GROUP, TILE)) * (
                            jnp.broadcast_to(reduced[j : j + 1], (GROUP, TILE))
                        )
                    pieces.append(piece)
                panel = jnp.concatenate(pieces, axis=0)
            total = jnp.where(below, 0.0, rest) - exact_dot(rest[:, :PANEL], panel)
            results.append(pltpu.roll(jnp.concatenate([total, panel], axis=0), TILE - PANEL, 1))
        return tuple(results)

    return lax.fori_loop(0, TILE // PANEL, step, tuple(tiles))


def exact_dot(a, b):
    return lax.dot_general(
        a, b, (((1,), (0,)), ((), ())), precision=lax.Precision.HIGHEST, preferred_element_type=jnp.float32
    )


def solve_systems(total, work, out, ridges, slots, per_fold, me):
    size = total.shape[0]
    traits = total.shape[1] - size
    eye = lax.broadcasted_iota(jnp.int32, (size, size), 0) == lax.broadcasted_iota(jnp.int32, (size, size), 1)
    for s in range(slots):
        level = lax.rem(lax.rem(me, per_fold) * slots + s, RIDGES)
        ridge = jnp.float32(ridges[0])
        for r in range(1, RIDGES):
            ridge = jnp.where(level == r, jnp.float32(ridges[r]), ridge)
        work[s, :, :size] = total[:, :size] + jnp.where(eye, ridge, 0.0)
        work[s, :, size:] = total[:, size:]
    for first in range(0, size, TILE):
        last = first + TILE
        inverses = invert_tiles([work[s, first:last, first:last] for s in range(slots)])
        for s in range(slots):
            scaled = exact_dot(inverses[s], work[s, first:last, last:])
            if first:
                work[s, :first, last:] = work[s, :first, last:] - exact_dot(work[s, :first, first:last], scaled)
            if last < size:
                work[s, last:, last:] = work[s, last:, last:] - exact_dot(work[s, last:, first:last], scaled)
            work[s, first:last, last:] = scaled
    for s in range(slots):
        out[s * traits : (s + 1) * traits, :] = work[s, :, size:].T.astype(out.dtype)


def layout(width):
    across = 2 if width == 16 else 1
    return width // (2 * across), across


def index_of(z, y, core, across):
    return (z * across + y) * 2 + core


def place_of(me, across):
    return me // (2 * across), lax.rem(me // 2, across), lax.rem(me, 2)


def copy_to(source, target, send, receive, device):
    return pltpu.make_async_remote_copy(
        src_ref=source,
        dst_ref=target,
        send_sem=send,
        recv_sem=receive,
        device_id={"ind": device},
        device_id_type=pl.DeviceIdType.MESH,
    )


def greet(partners, meanwhile):
    barrier = pltpu.get_barrier_semaphore()
    for exists, device in partners:

        @pl.when(exists)
        def _(device=device):
            pl.semaphore_signal(
                barrier, inc=1, device_id={"ind": device}, device_id_type=pl.DeviceIdType.MESH
            )

    meanwhile()
    expected = jnp.int32(0)
    for exists, _ in partners:
        expected = expected + exists.astype(jnp.int32)
    pl.semaphore_wait(barrier, expected)


UP, DOWN, ACROSS, SIBLING = range(4)


def spread(blocks, send, receive, width, use, needed):
    depth, across = layout(width)
    balanced = across > 1 and depth == 4
    rows = blocks.shape[1]
    cut = -(-rows // 32) * 16
    halves = ((0, cut), (cut, rows - cut))
    me = lax.axis_index("ind")
    z, y, core = place_of(me, across)
    first, last = z == 0, z == depth - 1
    sibling = index_of(z, y, 1 - core, across)
    opposite = index_of(z, lax.rem(y + 1, across), core, across)

    def copy(index, half, way):
        device = {
            UP: index_of(z + 1, y, core, across),
            DOWN: index_of(z - 1, y, core, across),
            ACROSS: opposite,
            SIBLING: sibling,
        }[way]
        piece = blocks.at[index, pl.ds(*halves[half])]
        return copy_to(piece, piece, send.at[way, index, half], receive.at[index, half], device)

    def arrived(index, half):
        copy(index, half, SIBLING).wait_recv()

    def line(step, side):
        origin = z + (2 * side - 1) * step
        valid = (step >= 0) & (origin >= 0) & (origin < depth) & ((step > 0) | (side == 0))
        return origin, valid

    def crossed_line(step, side):
        origin, valid = line(step, side)
        if not balanced:
            return origin, valid
        outer = (first & (side == 0)) | (last & (side == 1))
        late = outer & (step == depth - 1)
        skipped = (first | last) & (step == 1)
        inner = jnp.where(first, 1, depth - 2)
        return jnp.where(late, inner, origin), late | (valid & jnp.logical_not(skipped))

    def crosses(origin, half):
        if not balanced:
            return origin >= 0
        near = (origin == z - 1) | (origin == z + 1)
        ends = (origin == 0) | (origin == depth - 1)
        if half == 1:
            ends = ends | first | last
        return jnp.logical_not(near & ends)

    partner = index_of(z, lax.rem(y + 1, across), core, across)
    inner_ways = ((UP, first), (DOWN, last))
    outer_ways = ((DOWN, z == 1), (UP, z == depth - 2))

    def body(step, carry):
        for side in (0, 1):
            origin, valid = line(step, side)
            index = index_of(origin, y, core, across)

            @pl.when(valid)
            def _(index=index, side=side, origin=origin):
                for half in (0, 1):

                    @pl.when(needed(index, half))
                    def _(half=half):
                        @pl.when(step > 0)
                        def _():
                            arrived(index, half)

                        @pl.when(jnp.logical_not(last) if side == 0 else jnp.logical_not(first))
                        def _():
                            copy(index, half, UP if side == 0 else DOWN).start()

                        if side == 0:

                            @pl.when((step == 0) & (z > 0))
                            def _():
                                copy(index, half, DOWN).start()

                        if across > 1:

                            @pl.when(crosses(origin, half))
                            def _():
                                copy(index, half, ACROSS).start()

                        copy(index, half, SIBLING).start()

        if across > 1:
            for side in (0, 1):
                origin, valid = crossed_line(step - 1, side)
                index = index_of(origin, 1 - y, core, across)

                @pl.when(valid)
                def _(index=index):
                    for half in (0, 1):

                        @pl.when(needed(index, half))
                        def _(half=half):
                            arrived(index, half)
                            copy(index, half, SIBLING).start()

        if balanced:
            for way, here in inner_ways:

                for half in (0, 1):

                    @pl.when((step == 1) & here & needed(partner, half))
                    def _(way=way, half=half):
                        copy(partner, half, way).start()

            for way, here in outer_ways:

                @pl.when((step == 2) & here & needed(partner, 1))
                def _(way=way):
                    copy(partner, 1, way).start()

        def visit(turn, inner):
            side = lax.rem(turn, 2)
            crossed = lax.rem(turn // 2, across)
            shared = turn // (2 * across)
            when = step - crossed - shared
            origin, valid = line(when, side)
            if across > 1:
                other_origin, other_valid = crossed_line(when, side)
                origin = jnp.where(crossed == 1, other_origin, origin)
                valid = ((crossed == 1) & other_valid) | ((crossed == 0) & valid)
            index = index_of(origin, lax.rem(y + crossed, across), lax.rem(core + shared, 2), across)

            @pl.when(valid)
            def _():
                for half in (0, 1):

                    @pl.when((shared == 1) & needed(index, half))
                    def _(half=half):
                        arrived(index, half)

                use(index)

            return inner

        return lax.fori_loop(0, 4 * across, visit, carry) if use else carry

    lax.fori_loop(0, depth + across, body, 0)
    if not use:

        def collect(origin, carry):
            for there in range(across):
                index = index_of(origin, there, 1 - core, across)
                for half in (0, 1):

                    @pl.when(needed(index, half))
                    def _(index=index, half=half):
                        arrived(index, half)

            return carry

        lax.fori_loop(0, depth, collect, 0)

    def settle(origin, carry):
        own = index_of(origin, y, core, across)
        for half in (0, 1):

            wanted = needed(own, half)

            @pl.when(wanted & (z < depth - 1) & (origin <= z))
            def _():
                copy(own, half, UP).wait_send()

            @pl.when(wanted & (z > 0) & (origin >= z))
            def _():
                copy(own, half, DOWN).wait_send()

            @pl.when(wanted)
            def _():
                copy(own, half, SIBLING).wait_send()

            if across > 1:

                @pl.when(wanted & crosses(origin, half))
                def _():
                    copy(own, half, ACROSS).wait_send()

                other = index_of(origin, 1 - y, core, across)

                @pl.when(needed(other, half))
                def _():
                    copy(other, half, SIBLING).wait_send()
        return carry

    lax.fori_loop(0, depth, settle, 0)
    if balanced:
        for way, here in inner_ways:

            for half in (0, 1):

                @pl.when(here & needed(partner, half))
                def _(way=way, half=half):
                    copy(partner, half, way).wait_send()

        for way, here in outer_ways:

            @pl.when(here & needed(partner, 1))
            def _(way=way):
                copy(partner, 1, way).wait_send()


def spread_partners(width):
    depth, across = layout(width)
    me = lax.axis_index("ind")
    z, y, core = place_of(me, across)
    partners = [
        (z < depth - 1, index_of(z + 1, y, core, across)),
        (z > 0, index_of(z - 1, y, core, across)),
        (z >= 0, index_of(z, y, 1 - core, across)),
    ]
    if across > 1:
        partners.append((z >= 0, index_of(z, 1 - y, core, across)))
    return partners


def gram_kernel(width, per_fold, genotypes, phenotypes, folds, total, own, blocks, send, receive):
    me = lax.axis_index("ind")
    rows, size = total.shape[1], total.shape[0]
    fold = jnp.minimum(me // per_fold, FOLDS - 1).astype(jnp.float32)

    def prepare():
        members = folds[...].astype(jnp.float32)
        block = jnp.concatenate(
            [
                genotypes[...].T,
                phenotypes[...],
                jnp.broadcast_to(members, (EXTRA, members.shape[1])).astype(jnp.bfloat16),
            ],
            axis=0,
        )
        blocks[me] = block
        own[...] = block
        total[...] = jnp.zeros_like(total)

    greet(spread_partners(width), prepare)

    def use(index):
        keep = (blocks[index, rows : rows + EXTRA, :].astype(jnp.float32)[:1] != fold).astype(jnp.bfloat16)
        total[...] += lax.dot_general(
            blocks[index, :size, :] * keep,
            blocks[index, :rows, :],
            (((1,), (1,)), ((), ())),
            preferred_element_type=jnp.float32,
        )

    spread(blocks, send, receive, width, use, lambda index, half: index >= 0)


def leave_gram(genotypes, phenotypes, folds, width):
    individuals, size = genotypes.shape
    traits = phenotypes.shape[0]
    rows = size + traits + EXTRA
    per_fold, _ = plan(width)
    return pl.pallas_call(
        functools.partial(gram_kernel, width, per_fold),
        out_shape=(
            jax.ShapeDtypeStruct((size, size + traits), jnp.float32),
            jax.ShapeDtypeStruct((rows, individuals), jnp.bfloat16),
        ),
        scratch_shapes=[
            pltpu.VMEM((width, rows, individuals), jnp.bfloat16),
            pltpu.SemaphoreType.DMA((4, width, 2)),
            pltpu.SemaphoreType.DMA((width, 2)),
        ],
        compiler_params=pltpu.CompilerParams(
            collective_id=0,
            has_side_effects=True,
            vmem_limit_bytes=(14 << 20) + 2 * width * rows * individuals,
        ),
    )(genotypes, phenotypes, folds[None])


def small_solve(matrix, rhs):
    size = len(rhs)
    lower = {}
    for column in range(size):
        total = matrix[column][column]
        for inner in range(column):
            total = total - lower[column, inner] * lower[column, inner]
        lower[column, column] = jnp.sqrt(total)
        for row in range(column + 1, size):
            total = matrix[row][column]
            for inner in range(column):
                total = total - lower[row, inner] * lower[column, inner]
            lower[row, column] = total / lower[column, column]
    forward = []
    for row in range(size):
        total = rhs[row]
        for inner in range(row):
            total = total - lower[row, inner] * forward[inner]
        forward.append(total / lower[row, row])
    backward = {}
    for row in reversed(range(size)):
        total = forward[row]
        for inner in range(row + 1, size):
            total = total - lower[inner, row] * backward[inner]
        backward[row] = total / lower[row, row]
    return [backward[row] for row in range(size)]


def predict_kernel(
    width, per_fold, slots, ridges, system, block, raw, sums,
    work, coefficients, near, far, send, receive, near_send, near_receive, far_send, far_receive,
):
    size = coefficients.shape[2]
    traits = coefficients.shape[1] // slots
    rows = size + traits
    depth, across = layout(width)
    me = lax.axis_index("ind")
    z, y, core = place_of(me, across)
    corner = y * 2 + core
    near_devices = [(lax.rem(corner + k, 2 * across), k) for k in range(1, 2 * across)]
    far_devices = [(lax.rem(z + k, depth), k) for k in range(1, depth)]
    always = me >= 0
    geno = block[:size, :]
    phen = block[size:rows, :].astype(jnp.float32)
    folds = block[rows : rows + 1, :].astype(jnp.float32)

    def prepare():
        solve_systems(system, work, coefficients.at[me], ridges, slots, per_fold, me)

    greet(
        [(always, z * 2 * across + other) for other, _ in near_devices]
        + [(always, other * 2 * across + corner) for other, _ in far_devices],
        prepare,
    )
    cut = -(-slots * traits // 32) * 16

    def level_of(index, slot):
        return lax.rem(index, per_fold) * slots + slot

    def needed(index, half):
        return (index < FOLDS * per_fold) & (level_of(index, half * cut // traits) < RIDGES)

    spread(coefficients, send, receive, width, None, needed)
    total = None
    for fold in range(FOLDS):
        masked = geno * (folds == float(fold)).astype(jnp.bfloat16)
        flat = jnp.concatenate(
            [
                coefficients[fold * per_fold + r // slots, pl.ds(r % slots * traits, traits)]
                for r in range(RIDGES)
            ],
            axis=0,
        )
        part = lax.dot_general(flat, masked, (((1,), (0,)), ((), ())), preferred_element_type=jnp.float32)
        total = part if total is None else total + part
    raw[...] = total
    parts = [total[r * traits : (r + 1) * traits] for r in range(RIDGES)]
    lane = lax.broadcasted_iota(jnp.int32, (traits, TILE), 1)
    packed = jnp.zeros((traits, TILE), jnp.float32)
    place = 0
    for r in range(RIDGES):
        for other in parts[: r + 1] + [phen]:
            packed = jnp.where(lane == place, jnp.sum(parts[r] * other, axis=1, keepdims=True), packed)
            place += 1

    def exchange(buffer, mine, devices, sends, receives, device_of):
        copies = []
        for other, k in devices:
            copy = copy_to(
                buffer.at[mine], buffer.at[mine], sends.at[k], receives.at[mine], device_of(other)
            )
            copy.start()
            copies.append(copy)
        for other, k in devices:
            copy_to(
                buffer.at[other], buffer.at[other], sends.at[k], receives.at[other], device_of(other)
            ).wait_recv()
        for copy in copies:
            copy.wait_send()

    spare = jnp.zeros((SUMS, TILE - traits), jnp.float32)
    near[corner] = jnp.concatenate([packed.T[:SUMS], spare], axis=1)
    exchange(near, corner, near_devices, near_send, near_receive, lambda other: z * 2 * across + other)
    far[z] = jnp.sum(near[...], axis=0)
    exchange(far, z, far_devices, far_send, far_receive, lambda other: other * 2 * across + corner)
    gathered = jnp.sum(far[...], axis=0)
    filled = jnp.concatenate([gathered, jnp.zeros((TILE - SUMS, TILE), jnp.float32)], axis=0)
    sums[...] = filled.T[:traits]


def predict(system, own, ridges, width):
    size = system.shape[0]
    per_fold, slots = plan(width)
    traits = system.shape[1] - size
    depth, across = layout(width)
    return pl.pallas_call(
        functools.partial(predict_kernel, width, per_fold, slots, ridges),
        out_shape=(
            jax.ShapeDtypeStruct((RIDGES * traits, own.shape[1]), jnp.float32),
            jax.ShapeDtypeStruct((traits, TILE), jnp.float32),
        ),
        scratch_shapes=[
            pltpu.VMEM((slots, size, size + traits), jnp.float32),
            pltpu.VMEM((width, slots * traits, size), jnp.bfloat16),
            pltpu.VMEM((2 * across, SUMS, TILE), jnp.float32),
            pltpu.VMEM((depth, SUMS, TILE), jnp.float32),
            pltpu.SemaphoreType.DMA((4, width, 2)),
            pltpu.SemaphoreType.DMA((width, 2)),
            pltpu.SemaphoreType.DMA((2 * across,)),
            pltpu.SemaphoreType.DMA((2 * across,)),
            pltpu.SemaphoreType.DMA((depth,)),
            pltpu.SemaphoreType.DMA((depth,)),
        ],
        compiler_params=pltpu.CompilerParams(
            collective_id=1, has_side_effects=True, vmem_limit_bytes=40 << 20
        ),
    )(system, own)


def finish_kernel(count, ridges, sums, raw, block, stacked):
    traits = sums.shape[0]
    gram = {}
    cross = []
    place = 0
    for r in range(RIDGES):
        for s in range(r + 1):
            gram[r, s] = sums[:, place : place + 1]
            place += 1
        cross.append(sums[:, place : place + 1])
        place += 1
    scale = [1.0 / jnp.sqrt(gram[r, r] / count + epsilon) for r in range(RIDGES)]
    lane = lax.broadcasted_iota(jnp.int32, (traits, TILE), 1)
    ridge = jnp.full((traits, TILE), ridges[0], jnp.float32)
    for s in range(1, RIDGES):
        ridge = jnp.where(lane == s, ridges[s], ridge)
    matrix = [
        [
            jnp.broadcast_to(gram[r, s] * scale[r] * scale[s], (traits, TILE)) + (ridge if r == s else 0.0)
            if s <= r
            else None
            for s in range(RIDGES)
        ]
        for r in range(RIDGES)
    ]
    rhs = [jnp.broadcast_to(cross[r] * scale[r], (traits, TILE)) for r in range(RIDGES)]
    weights = small_solve(matrix, rhs)
    parts = []
    for r in range(RIDGES):
        part = raw[r * traits : (r + 1) * traits, :] * scale[r]
        block[r] = part
        parts.append(part)
    for s in range(RIDGES):
        total = weights[0][:, s : s + 1] * parts[0]
        for r in range(1, RIDGES):
            total = total + weights[r][:, s : s + 1] * parts[r]
        stacked[s] = total


def shards(genotypes, phenotypes, folds):
    rows = genotypes.shape[0]
    traits = phenotypes.shape[0]
    width = lax.axis_size("ind")
    count = rows * width
    ridges = ridge_list(count)
    total, own = leave_gram(genotypes, phenotypes, folds, width)
    raw, sums = predict(total, own, ridges, width)
    shape = jax.ShapeDtypeStruct((RIDGES, traits, rows), jnp.float32)
    return pl.pallas_call(
        functools.partial(finish_kernel, count, ridges),
        out_shape=(shape, shape),
        compiler_params=pltpu.CompilerParams(vmem_limit_bytes=40 << 20),
    )(sums, raw)


def solution(mesh):
    placed = (P(("cohort", "ind"), None), P(None, ("cohort", "ind")), P(("cohort", "ind")))
    return jax.shard_map(
        shards,
        mesh=mesh,
        in_specs=placed,
        out_specs=(P(None, None, ("cohort", "ind")), P(None, None, ("cohort", "ind"))),
        check_vma=False,
    )
```

```python
import functools

import jax
import jax.numpy as jnp
import numpy as np
from jax import lax
from jax.experimental import pallas as pl
from jax.experimental.pallas import tpu as pltpu
from jax.sharding import PartitionSpec as P

FOLDS = 5
RIDGES = 5
TILE = 128
GROUP = 8
PANEL = 16
SUMS = 24
EXTRA = 16

heritability = (0.01, 0.25, 0.5, 0.75, 0.99)
epsilon = 1e-06


def ridge_list(count):
    shares = np.asarray(heritability, np.float32)
    return [float(v) for v in np.float32(count) * (np.float32(1.0) - shares) / shares]


def plan(width):
    per_fold = min(width // FOLDS, RIDGES)
    slots = (RIDGES + per_fold - 1) // per_fold
    return per_fold, slots


def eliminate_eight(panel, at, row, lane):
    head = panel[at : at + GROUP]
    columns = [jnp.broadcast_to(head[:, at + j : at + j + 1], (GROUP, TILE)) for j in range(GROUP)]
    inside = (lane >= at) & (lane < at + GROUP)
    reduced = jnp.where(inside, jnp.where(lane - at == row, 1.0, 0.0), head)
    for p in range(GROUP):
        column = columns[p]
        inverse = 1.0 / jnp.broadcast_to(column[p : p + 1], (GROUP, TILE))
        here = row == p

        def eliminate(value):
            pivot = jnp.broadcast_to(value[p : p + 1], (GROUP, TILE))
            return jnp.where(here, pivot * inverse, value - (column * pivot) * inverse)

        reduced = eliminate(reduced)
        for j in range(p + 1, GROUP):
            columns[j] = eliminate(columns[j])
    return reduced


def invert_tiles(tiles):
    lane = lax.broadcasted_iota(jnp.int32, (GROUP, TILE), 1)
    row = lax.broadcasted_iota(jnp.int32, (GROUP, TILE), 0)
    below = lax.broadcasted_iota(jnp.int32, (TILE - PANEL, TILE), 1) < PANEL

    def step(_, tiles):
        results = []
        for tile in tiles:
            panel, rest = tile[:PANEL], tile[PANEL:]
            for at in range(0, PANEL, GROUP):
                reduced = eliminate_eight(panel, at, row, lane)
                pieces = []
                for other in range(0, PANEL, GROUP):
                    if other == at:
                        pieces.append(reduced)
                        continue
                    old = panel[other : other + GROUP]
                    piece = jnp.where((lane >= at) & (lane < at + GROUP), 0.0, old)
                    for j in range(GROUP):
                        piece = piece - jnp.broadcast_to(old[:, at + j : at + j + 1], (GROUP, TILE)) * (
                            jnp.broadcast_to(reduced[j : j + 1], (GROUP, TILE))
                        )
                    pieces.append(piece)
                panel = jnp.concatenate(pieces, axis=0)
            total = jnp.where(below, 0.0, rest) - exact_dot(rest[:, :PANEL], panel)
            results.append(pltpu.roll(jnp.concatenate([total, panel], axis=0), TILE - PANEL, 1))
        return tuple(results)

    return lax.fori_loop(0, TILE // PANEL, step, tuple(tiles))


def exact_dot(a, b):
    return lax.dot_general(
        a, b, (((1,), (0,)), ((), ())), precision=lax.Precision.HIGHEST, preferred_element_type=jnp.float32
    )


def solve_systems(total, work, out, ridges, slots, per_fold, me):
    size = total.shape[0]
    traits = total.shape[1] - size
    eye = lax.broadcasted_iota(jnp.int32, (size, size), 0) == lax.broadcasted_iota(jnp.int32, (size, size), 1)
    for s in range(slots):
        level = lax.rem(lax.rem(me, per_fold) * slots + s, RIDGES)
        ridge = jnp.float32(ridges[0])
        for r in range(1, RIDGES):
            ridge = jnp.where(level == r, jnp.float32(ridges[r]), ridge)
        work[s, :, :size] = total[:, :size] + jnp.where(eye, ridge, 0.0)
        work[s, :, size:] = total[:, size:]
    for first in range(0, size, TILE):
        last = first + TILE
        inverses = invert_tiles([work[s, first:last, first:last] for s in range(slots)])
        for s in range(slots):
            scaled = exact_dot(inverses[s], work[s, first:last, last:])
            if first:
                work[s, :first, last:] = work[s, :first, last:] - exact_dot(work[s, :first, first:last], scaled)
            if last < size:
                work[s, last:, last:] = work[s, last:, last:] - exact_dot(work[s, last:, first:last], scaled)
            work[s, first:last, last:] = scaled
    for s in range(slots):
        out[s * traits : (s + 1) * traits, :] = work[s, :, size:].T.astype(out.dtype)


def layout(width):
    across = 2 if width == 16 else 1
    return width // (2 * across), across


def index_of(z, y, core, across):
    return (z * across + y) * 2 + core


def place_of(me, across):
    return me // (2 * across), lax.rem(me // 2, across), lax.rem(me, 2)


def copy_to(source, target, send, receive, device):
    return pltpu.make_async_remote_copy(
        src_ref=source,
        dst_ref=target,
        send_sem=send,
        recv_sem=receive,
        device_id={"ind": device},
        device_id_type=pl.DeviceIdType.MESH,
    )


def greet(partners, meanwhile):
    barrier = pltpu.get_barrier_semaphore()
    for exists, device in partners:

        @pl.when(exists)
        def _(device=device):
            pl.semaphore_signal(
                barrier, inc=1, device_id={"ind": device}, device_id_type=pl.DeviceIdType.MESH
            )

    meanwhile()
    expected = jnp.int32(0)
    for exists, _ in partners:
        expected = expected + exists.astype(jnp.int32)
    pl.semaphore_wait(barrier, expected)


UP, DOWN, ACROSS, SIBLING = range(4)


def spread(blocks, send, receive, width, use, needed, direct):
    depth, across = layout(width)
    balanced = across > 1 and depth == 4 and not direct
    rows = blocks.shape[1]
    cut = -(-rows // 32) * 16
    halves = ((0, cut), (cut, rows - cut))
    me = lax.axis_index("ind")
    z, y, core = place_of(me, across)
    first, last = z == 0, z == depth - 1
    sibling = index_of(z, y, 1 - core, across)
    opposite = index_of(z, lax.rem(y + 1, across), core, across)

    def copy(index, half, way):
        device = {
            UP: index_of(z + 1, y, core, across),
            DOWN: index_of(z - 1, y, core, across),
            ACROSS: opposite,
            SIBLING: sibling,
        }[way]
        piece = blocks.at[index, pl.ds(*halves[half])]
        return copy_to(piece, piece, send.at[way, index, half], receive.at[index, half], device)

    def straight(target, half):
        device = index_of(target, y, core, across)
        piece = blocks.at[me, pl.ds(*halves[half])]
        return copy_to(piece, piece, send.at[UP, device, half], receive.at[me, half], device)

    def arrived(index, half):
        copy(index, half, SIBLING).wait_recv()

    def line(step, side):
        origin = z + (2 * side - 1) * step
        valid = (step >= 0) & (origin >= 0) & (origin < depth) & ((step > 0) | (side == 0))
        return origin, valid

    def crossed_line(step, side):
        origin, valid = line(step, side)
        if not balanced:
            return origin, valid
        outer = (first & (side == 0)) | (last & (side == 1))
        late = outer & (step == depth - 1)
        skipped = (first | last) & (step == 1)
        inner = jnp.where(first, 1, depth - 2)
        return jnp.where(late, inner, origin), late | (valid & jnp.logical_not(skipped))

    def crosses(origin, half):
        if not balanced:
            return origin >= 0
        near = (origin == z - 1) | (origin == z + 1)
        ends = (origin == 0) | (origin == depth - 1)
        if half == 1:
            ends = ends | first | last
        return jnp.logical_not(near & ends)

    partner = index_of(z, lax.rem(y + 1, across), core, across)
    inner_ways = ((UP, first), (DOWN, last))
    outer_ways = ((DOWN, z == 1), (UP, z == depth - 2))

    def body(step, carry):
        for side in (0, 1):
            origin, valid = line(step, side)
            index = index_of(origin, y, core, across)

            @pl.when(valid)
            def _(index=index, side=side, origin=origin):
                for half in (0, 1):

                    @pl.when(needed(index, half))
                    def _(half=half):
                        @pl.when(step > 0)
                        def _():
                            arrived(index, half)

                        if not direct:

                            @pl.when(jnp.logical_not(last) if side == 0 else jnp.logical_not(first))
                            def _():
                                copy(index, half, UP if side == 0 else DOWN).start()

                        if direct and side == 0:

                            @pl.when(step == 0)
                            def _():
                                for k in range(depth - 1, 0, -1):
                                    straight(lax.rem(z + k, depth), half).start()

                        elif side == 0:

                            @pl.when((step == 0) & (z > 0))
                            def _():
                                copy(index, half, DOWN).start()

                        if across > 1:

                            @pl.when(crosses(origin, half))
                            def _():
                                copy(index, half, ACROSS).start()

                        copy(index, half, SIBLING).start()

        if across > 1:
            for side in (0, 1):
                origin, valid = crossed_line(step - 1, side)
                index = index_of(origin, 1 - y, core, across)

                @pl.when(valid)
                def _(index=index):
                    for half in (0, 1):

                        @pl.when(needed(index, half))
                        def _(half=half):
                            arrived(index, half)
                            copy(index, half, SIBLING).start()

        if balanced:
            for way, here in inner_ways:

                for half in (0, 1):

                    @pl.when((step == 1) & here & needed(partner, half))
                    def _(way=way, half=half):
                        copy(partner, half, way).start()

            for way, here in outer_ways:

                @pl.when((step == 2) & here & needed(partner, 1))
                def _(way=way):
                    copy(partner, 1, way).start()

        def visit(turn, inner):
            side = lax.rem(turn, 2)
            crossed = lax.rem(turn // 2, across)
            shared = turn // (2 * across)
            when = step - crossed - shared
            origin, valid = line(when, side)
            if across > 1:
                other_origin, other_valid = crossed_line(when, side)
                origin = jnp.where(crossed == 1, other_origin, origin)
                valid = ((crossed == 1) & other_valid) | ((crossed == 0) & valid)
            index = index_of(origin, lax.rem(y + crossed, across), lax.rem(core + shared, 2), across)

            @pl.when(valid)
            def _():
                for half in (0, 1):

                    @pl.when((shared == 1) & needed(index, half))
                    def _(half=half):
                        arrived(index, half)

                use(index)

            return inner

        return lax.fori_loop(0, 4 * across, visit, carry) if use else carry

    lax.fori_loop(0, depth + across, body, 0)
    if not use:

        def collect(origin, carry):
            for there in range(across):
                index = index_of(origin, there, 1 - core, across)
                for half in (0, 1):

                    @pl.when(needed(index, half))
                    def _(index=index, half=half):
                        arrived(index, half)

            return carry

        lax.fori_loop(0, depth, collect, 0)

    def settle(origin, carry):
        own = index_of(origin, y, core, across)
        for half in (0, 1):

            wanted = needed(own, half)

            if direct:

                @pl.when(needed(me, half) & (origin != z))
                def _():
                    straight(origin, half).wait_send()

            else:

                @pl.when(wanted & (z < depth - 1) & (origin <= z))
                def _():
                    copy(own, half, UP).wait_send()

                @pl.when(wanted & (z > 0) & (origin >= z))
                def _():
                    copy(own, half, DOWN).wait_send()

            @pl.when(wanted)
            def _():
                copy(own, half, SIBLING).wait_send()

            if across > 1:

                @pl.when(wanted & crosses(origin, half))
                def _():
                    copy(own, half, ACROSS).wait_send()

                other = index_of(origin, 1 - y, core, across)

                @pl.when(needed(other, half))
                def _():
                    copy(other, half, SIBLING).wait_send()
        return carry

    lax.fori_loop(0, depth, settle, 0)
    if balanced:
        for way, here in inner_ways:

            for half in (0, 1):

                @pl.when(here & needed(partner, half))
                def _(way=way, half=half):
                    copy(partner, half, way).wait_send()

        for way, here in outer_ways:

            @pl.when(here & needed(partner, 1))
            def _(way=way):
                copy(partner, 1, way).wait_send()


def spread_partners(width):
    depth, across = layout(width)
    me = lax.axis_index("ind")
    z, y, core = place_of(me, across)
    partners = [
        (z < depth - 1, index_of(z + 1, y, core, across)),
        (z > 0, index_of(z - 1, y, core, across)),
        (z >= 0, index_of(z, y, 1 - core, across)),
    ]
    if across > 1:
        partners.append((z >= 0, index_of(z, 1 - y, core, across)))
    return partners


def gram_kernel(
    width, per_fold, genotypes_in, phenotypes_in, folds_in, total, own,
    blocks, send, receive, genotypes, phenotypes, folds, arrivals,
):
    me = lax.axis_index("ind")
    rows, size = total.shape[1], total.shape[0]
    fold = jnp.minimum(me // per_fold, FOLDS - 1).astype(jnp.float32)

    pairs = ((genotypes_in, genotypes), (phenotypes_in, phenotypes), (folds_in, folds))
    fills = [pltpu.make_async_copy(a, b, arrivals.at[i]) for i, (a, b) in enumerate(pairs)]
    for fill in fills:
        fill.start()

    def prepare():
        total[...] = jnp.zeros_like(total)
        for fill in fills:
            fill.wait()
        members = folds[...].astype(jnp.float32)
        block = jnp.concatenate(
            [
                genotypes[...].T,
                phenotypes[...],
                jnp.broadcast_to(members, (EXTRA, members.shape[1])).astype(jnp.bfloat16),
            ],
            axis=0,
        )
        blocks[me] = block
        own[...] = block

    greet(spread_partners(width), prepare)

    def use(index):
        keep = (blocks[index, rows : rows + EXTRA, :].astype(jnp.float32)[:1] != fold).astype(jnp.bfloat16)
        total[...] += lax.dot_general(
            blocks[index, :size, :] * keep,
            blocks[index, :rows, :],
            (((1,), (1,)), ((), ())),
            preferred_element_type=jnp.float32,
        )

    spread(blocks, send, receive, width, use, lambda index, half: index >= 0, False)


def leave_gram(genotypes, phenotypes, folds, width):
    individuals, size = genotypes.shape
    traits = phenotypes.shape[0]
    rows = size + traits + EXTRA
    per_fold, _ = plan(width)
    return pl.pallas_call(
        functools.partial(gram_kernel, width, per_fold),
        out_shape=(
            jax.ShapeDtypeStruct((size, size + traits), jnp.float32),
            jax.ShapeDtypeStruct((rows, individuals), jnp.bfloat16),
        ),
        in_specs=[pl.BlockSpec(memory_space=pl.ANY)] * 3,
        scratch_shapes=[
            pltpu.VMEM((width, rows, individuals), jnp.bfloat16),
            pltpu.SemaphoreType.DMA((4, width, 2)),
            pltpu.SemaphoreType.DMA((width, 2)),
            pltpu.VMEM(genotypes.shape, jnp.bfloat16),
            pltpu.VMEM(phenotypes.shape, jnp.bfloat16),
            pltpu.VMEM((1, individuals), jnp.int32),
            pltpu.SemaphoreType.DMA((3,)),
        ],
        compiler_params=pltpu.CompilerParams(
            collective_id=0,
            has_side_effects=True,
            vmem_limit_bytes=(15 << 20) + 2 * width * rows * individuals,
        ),
    )(genotypes, phenotypes, folds[None])


def small_solve(matrix, rhs):
    size = len(rhs)
    lower = {}
    for column in range(size):
        total = matrix[column][column]
        for inner in range(column):
            total = total - lower[column, inner] * lower[column, inner]
        lower[column, column] = jnp.sqrt(total)
        for row in range(column + 1, size):
            total = matrix[row][column]
            for inner in range(column):
                total = total - lower[row, inner] * lower[column, inner]
            lower[row, column] = total / lower[column, column]
    forward = []
    for row in range(size):
        total = rhs[row]
        for inner in range(row):
            total = total - lower[row, inner] * forward[inner]
        forward.append(total / lower[row, row])
    backward = {}
    for row in reversed(range(size)):
        total = forward[row]
        for inner in range(row + 1, size):
            total = total - lower[inner, row] * backward[inner]
        backward[row] = total / lower[row, row]
    return [backward[row] for row in range(size)]


def predict_kernel(
    width, per_fold, slots, ridges, system, block, raw, sums,
    work, coefficients, near, far, send, receive, near_send, near_receive, far_send, far_receive,
):
    size = coefficients.shape[2]
    traits = coefficients.shape[1] // slots
    rows = size + traits
    depth, across = layout(width)
    me = lax.axis_index("ind")
    z, y, core = place_of(me, across)
    corner = y * 2 + core
    near_devices = [(lax.rem(corner + k, 2 * across), k) for k in range(1, 2 * across)]
    far_devices = [(lax.rem(z + k, depth), k) for k in range(1, depth)]
    always = me >= 0
    geno = block[:size, :]
    phen = block[size:rows, :].astype(jnp.float32)
    folds = block[rows : rows + 1, :].astype(jnp.float32)

    def prepare():
        solve_systems(system, work, coefficients.at[me], ridges, slots, per_fold, me)

    greet(
        [(always, z * 2 * across + other) for other, _ in near_devices]
        + [(always, other * 2 * across + corner) for other, _ in far_devices],
        prepare,
    )
    cut = -(-slots * traits // 32) * 16

    def level_of(index, slot):
        return lax.rem(index, per_fold) * slots + slot

    def needed(index, half):
        return (index < FOLDS * per_fold) & (level_of(index, half * cut // traits) < RIDGES)

    spread(coefficients, send, receive, width, None, needed, True)
    total = None
    for fold in range(FOLDS):
        masked = geno * (folds == float(fold)).astype(jnp.bfloat16)
        flat = jnp.concatenate(
            [
                coefficients[fold * per_fold + r // slots, pl.ds(r % slots * traits, traits)]
                for r in range(RIDGES)
            ],
            axis=0,
        )
        part = lax.dot_general(flat, masked, (((1,), (0,)), ((), ())), preferred_element_type=jnp.float32)
        total = part if total is None else total + part
    raw[...] = total
    parts = [total[r * traits : (r + 1) * traits] for r in range(RIDGES)]
    lane = lax.broadcasted_iota(jnp.int32, (traits, TILE), 1)
    packed = jnp.zeros((traits, TILE), jnp.float32)
    place = 0
    for r in range(RIDGES):
        for other in parts[: r + 1] + [phen]:
            packed = jnp.where(lane == place, jnp.sum(parts[r] * other, axis=1, keepdims=True), packed)
            place += 1

    def exchange(buffer, mine, devices, sends, receives, device_of):
        copies = []
        for other, k in devices:
            copy = copy_to(
                buffer.at[mine], buffer.at[mine], sends.at[k], receives.at[mine], device_of(other)
            )
            copy.start()
            copies.append(copy)
        for other, k in devices:
            copy_to(
                buffer.at[other], buffer.at[other], sends.at[k], receives.at[other], device_of(other)
            ).wait_recv()
        for copy in copies:
            copy.wait_send()

    spare = jnp.zeros((SUMS, TILE - traits), jnp.float32)
    near[corner] = jnp.concatenate([packed.T[:SUMS], spare], axis=1)
    exchange(near, corner, near_devices, near_send, near_receive, lambda other: z * 2 * across + other)
    far[z] = jnp.sum(near[...], axis=0)
    exchange(far, z, far_devices, far_send, far_receive, lambda other: other * 2 * across + corner)
    gathered = jnp.sum(far[...], axis=0)
    filled = jnp.concatenate([gathered, jnp.zeros((TILE - SUMS, TILE), jnp.float32)], axis=0)
    sums[...] = filled.T[:traits]


def predict(system, own, ridges, width):
    size = system.shape[0]
    per_fold, slots = plan(width)
    traits = system.shape[1] - size
    depth, across = layout(width)
    return pl.pallas_call(
        functools.partial(predict_kernel, width, per_fold, slots, ridges),
        out_shape=(
            jax.ShapeDtypeStruct((RIDGES * traits, own.shape[1]), jnp.float32),
            jax.ShapeDtypeStruct((traits, TILE), jnp.float32),
        ),
        scratch_shapes=[
            pltpu.VMEM((slots, size, size + traits), jnp.float32),
            pltpu.VMEM((width, slots * traits, size), jnp.bfloat16),
            pltpu.VMEM((2 * across, SUMS, TILE), jnp.float32),
            pltpu.VMEM((depth, SUMS, TILE), jnp.float32),
            pltpu.SemaphoreType.DMA((4, width, 2)),
            pltpu.SemaphoreType.DMA((width, 2)),
            pltpu.SemaphoreType.DMA((2 * across,)),
            pltpu.SemaphoreType.DMA((2 * across,)),
            pltpu.SemaphoreType.DMA((depth,)),
            pltpu.SemaphoreType.DMA((depth,)),
        ],
        compiler_params=pltpu.CompilerParams(
            collective_id=1, has_side_effects=True, vmem_limit_bytes=40 << 20
        ),
    )(system, own)


def finish_kernel(count, ridges, sums, raw, block, stacked):
    traits = sums.shape[0]
    gram = {}
    cross = []
    place = 0
    for r in range(RIDGES):
        for s in range(r + 1):
            gram[r, s] = sums[:, place : place + 1]
            place += 1
        cross.append(sums[:, place : place + 1])
        place += 1
    scale = [1.0 / jnp.sqrt(gram[r, r] / count + epsilon) for r in range(RIDGES)]
    lane = lax.broadcasted_iota(jnp.int32, (traits, TILE), 1)
    ridge = jnp.full((traits, TILE), ridges[0], jnp.float32)
    for s in range(1, RIDGES):
        ridge = jnp.where(lane == s, ridges[s], ridge)
    matrix = [
        [
            jnp.broadcast_to(gram[r, s] * scale[r] * scale[s], (traits, TILE)) + (ridge if r == s else 0.0)
            if s <= r
            else None
            for s in range(RIDGES)
        ]
        for r in range(RIDGES)
    ]
    rhs = [jnp.broadcast_to(cross[r] * scale[r], (traits, TILE)) for r in range(RIDGES)]
    weights = small_solve(matrix, rhs)
    parts = []
    for r in range(RIDGES):
        part = raw[r * traits : (r + 1) * traits, :] * scale[r]
        block[r] = part
        parts.append(part)
    for s in range(RIDGES):
        total = weights[0][:, s : s + 1] * parts[0]
        for r in range(1, RIDGES):
            total = total + weights[r][:, s : s + 1] * parts[r]
        stacked[s] = total


def shards(genotypes, phenotypes, folds):
    rows = genotypes.shape[0]
    traits = phenotypes.shape[0]
    width = lax.axis_size("ind")
    count = rows * width
    ridges = ridge_list(count)
    total, own = leave_gram(genotypes, phenotypes, folds, width)
    raw, sums = predict(total, own, ridges, width)
    shape = jax.ShapeDtypeStruct((RIDGES, traits, rows), jnp.float32)
    return pl.pallas_call(
        functools.partial(finish_kernel, count, ridges),
        out_shape=(shape, shape),
        compiler_params=pltpu.CompilerParams(vmem_limit_bytes=40 << 20),
    )(sums, raw)


def solution(mesh):
    placed = (P(("cohort", "ind"), None), P(None, ("cohort", "ind")), P(("cohort", "ind")))
    return jax.shard_map(
        shards,
        mesh=mesh,
        in_specs=placed,
        out_specs=(P(None, None, ("cohort", "ind")), P(None, None, ("cohort", "ind"))),
        check_vma=False,
    )
```

```python
import functools

import jax
import jax.numpy as jnp
import numpy as np
from jax import lax
from jax.experimental import pallas as pl
from jax.experimental.pallas import tpu as pltpu
from jax.sharding import PartitionSpec as P

FOLDS = 5
RIDGES = 5
TILE = 128
GROUP = 8
PANEL = 16
SUMS = 24
PIECES = 4
EXTRA = 16

heritability = (0.01, 0.25, 0.5, 0.75, 0.99)
epsilon = 1e-06


def ridge_list(count):
    shares = np.asarray(heritability, np.float32)
    return [float(v) for v in np.float32(count) * (np.float32(1.0) - shares) / shares]


def plan(width):
    per_fold = min(width // FOLDS, RIDGES)
    slots = (RIDGES + per_fold - 1) // per_fold
    return per_fold, slots


def eliminate_eight(panel, at, row, lane):
    head = panel[at : at + GROUP]
    columns = [jnp.broadcast_to(head[:, at + j : at + j + 1], (GROUP, TILE)) for j in range(GROUP)]
    inside = (lane >= at) & (lane < at + GROUP)
    reduced = jnp.where(inside, jnp.where(lane - at == row, 1.0, 0.0), head)
    for p in range(GROUP):
        column = columns[p]
        inverse = 1.0 / jnp.broadcast_to(column[p : p + 1], (GROUP, TILE))
        here = row == p

        def eliminate(value):
            pivot = jnp.broadcast_to(value[p : p + 1], (GROUP, TILE))
            return jnp.where(here, pivot * inverse, value - (column * pivot) * inverse)

        reduced = eliminate(reduced)
        for j in range(p + 1, GROUP):
            columns[j] = eliminate(columns[j])
    return reduced


def invert_tiles(tiles):
    lane = lax.broadcasted_iota(jnp.int32, (GROUP, TILE), 1)
    row = lax.broadcasted_iota(jnp.int32, (GROUP, TILE), 0)
    below = lax.broadcasted_iota(jnp.int32, (TILE - PANEL, TILE), 1) < PANEL

    def step(_, tiles):
        results = []
        for tile in tiles:
            panel, rest = tile[:PANEL], tile[PANEL:]
            for at in range(0, PANEL, GROUP):
                reduced = eliminate_eight(panel, at, row, lane)
                pieces = []
                for other in range(0, PANEL, GROUP):
                    if other == at:
                        pieces.append(reduced)
                        continue
                    old = panel[other : other + GROUP]
                    piece = jnp.where((lane >= at) & (lane < at + GROUP), 0.0, old)
                    for j in range(GROUP):
                        piece = piece - jnp.broadcast_to(old[:, at + j : at + j + 1], (GROUP, TILE)) * (
                            jnp.broadcast_to(reduced[j : j + 1], (GROUP, TILE))
                        )
                    pieces.append(piece)
                panel = jnp.concatenate(pieces, axis=0)
            total = jnp.where(below, 0.0, rest) - exact_dot(rest[:, :PANEL], panel)
            results.append(pltpu.roll(jnp.concatenate([total, panel], axis=0), TILE - PANEL, 1))
        return tuple(results)

    return lax.fori_loop(0, TILE // PANEL, step, tuple(tiles))


def exact_dot(a, b):
    return lax.dot_general(
        a, b, (((1,), (0,)), ((), ())), precision=lax.Precision.HIGHEST, preferred_element_type=jnp.float32
    )


def solve_systems(total, work, out, ridges, slots, per_fold, me):
    size = total.shape[0]
    traits = total.shape[1] - size
    eye = lax.broadcasted_iota(jnp.int32, (size, size), 0) == lax.broadcasted_iota(jnp.int32, (size, size), 1)
    for s in range(slots):
        level = lax.rem(lax.rem(me, per_fold) * slots + s, RIDGES)
        ridge = jnp.float32(ridges[0])
        for r in range(1, RIDGES):
            ridge = jnp.where(level == r, jnp.float32(ridges[r]), ridge)
        work[s, :, :size] = total[:, :size] + jnp.where(eye, ridge, 0.0)
        work[s, :, size:] = total[:, size:]
    for first in range(0, size, TILE):
        last = first + TILE
        inverses = invert_tiles([work[s, first:last, first:last] for s in range(slots)])
        for s in range(slots):
            scaled = exact_dot(inverses[s], work[s, first:last, last:])
            if first:
                work[s, :first, last:] = work[s, :first, last:] - exact_dot(work[s, :first, first:last], scaled)
            if last < size:
                work[s, last:, last:] = work[s, last:, last:] - exact_dot(work[s, last:, first:last], scaled)
            work[s, first:last, last:] = scaled
    for s in range(slots):
        out[s * traits : (s + 1) * traits, :] = work[s, :, size:].T.astype(out.dtype)


def layout(width):
    across = 2 if width == 16 else 1
    return width // (2 * across), across


def index_of(z, y, core, across):
    return (z * across + y) * 2 + core


def place_of(me, across):
    return me // (2 * across), lax.rem(me // 2, across), lax.rem(me, 2)


def copy_to(source, target, send, receive, device):
    return pltpu.make_async_remote_copy(
        src_ref=source,
        dst_ref=target,
        send_sem=send,
        recv_sem=receive,
        device_id={"ind": device},
        device_id_type=pl.DeviceIdType.MESH,
    )


def greet(partners, meanwhile):
    barrier = pltpu.get_barrier_semaphore()
    for exists, device in partners:

        @pl.when(exists)
        def _(device=device):
            pl.semaphore_signal(
                barrier, inc=1, device_id={"ind": device}, device_id_type=pl.DeviceIdType.MESH
            )

    meanwhile()
    expected = jnp.int32(0)
    for exists, _ in partners:
        expected = expected + exists.astype(jnp.int32)
    pl.semaphore_wait(barrier, expected)


UP, DOWN, ACROSS, SIBLING = range(4)


def spread(blocks, send, receive, width, use, needed, direct):
    depth, across = layout(width)
    balanced = across > 1 and depth == 4 and not direct
    rows = blocks.shape[1]
    parts = receive.shape[1]
    cut = -(-rows // (16 * parts)) * 16
    halves = [(cut * i, min(cut, rows - cut * i)) for i in range(parts)]
    late_halves = range(parts // 2, parts)
    me = lax.axis_index("ind")
    z, y, core = place_of(me, across)
    first, last = z == 0, z == depth - 1
    sibling = index_of(z, y, 1 - core, across)
    opposite = index_of(z, lax.rem(y + 1, across), core, across)

    def copy(index, half, way):
        device = {
            UP: index_of(z + 1, y, core, across),
            DOWN: index_of(z - 1, y, core, across),
            ACROSS: opposite,
            SIBLING: sibling,
        }[way]
        piece = blocks.at[index, pl.ds(*halves[half])]
        return copy_to(piece, piece, send.at[way, index, half], receive.at[index, half], device)

    def straight(target, half):
        device = index_of(target, y, core, across)
        piece = blocks.at[me, pl.ds(*halves[half])]
        return copy_to(piece, piece, send.at[UP, device, half], receive.at[me, half], device)

    def arrived(index, half):
        copy(index, half, SIBLING).wait_recv()

    def line(step, side):
        origin = z + (2 * side - 1) * step
        valid = (step >= 0) & (origin >= 0) & (origin < depth) & ((step > 0) | (side == 0))
        return origin, valid

    def crossed_line(step, side):
        origin, valid = line(step, side)
        if not balanced:
            return origin, valid
        outer = (first & (side == 0)) | (last & (side == 1))
        late = outer & (step == depth - 1)
        skipped = (first | last) & (step == 1)
        inner = jnp.where(first, 1, depth - 2)
        return jnp.where(late, inner, origin), late | (valid & jnp.logical_not(skipped))

    def crosses(origin, half):
        if not balanced:
            return origin >= 0
        near = (origin == z - 1) | (origin == z + 1)
        ends = (origin == 0) | (origin == depth - 1)
        if half in late_halves:
            ends = ends | first | last
        return jnp.logical_not(near & ends)

    partner = index_of(z, lax.rem(y + 1, across), core, across)
    inner_ways = ((UP, first), (DOWN, last))
    outer_ways = ((DOWN, z == 1), (UP, z == depth - 2))

    def body(step, carry):
        for side in (0, 1):
            origin, valid = line(step, side)
            index = index_of(origin, y, core, across)

            @pl.when(valid)
            def _(index=index, side=side, origin=origin):
                for half in range(parts):

                    @pl.when(needed(index, half))
                    def _(half=half):
                        @pl.when(step > 0)
                        def _():
                            arrived(index, half)

                        if not direct:

                            @pl.when(jnp.logical_not(last) if side == 0 else jnp.logical_not(first))
                            def _():
                                copy(index, half, UP if side == 0 else DOWN).start()

                        if direct and side == 0:

                            @pl.when(step == 0)
                            def _():
                                for k in range(depth - 1, 0, -1):
                                    straight(lax.rem(z + k, depth), half).start()

                        elif side == 0:

                            @pl.when((step == 0) & (z > 0))
                            def _():
                                copy(index, half, DOWN).start()

                        if across > 1:

                            @pl.when(crosses(origin, half))
                            def _():
                                copy(index, half, ACROSS).start()

                        copy(index, half, SIBLING).start()

        if across > 1:
            for side in (0, 1):
                origin, valid = crossed_line(step - 1, side)
                index = index_of(origin, 1 - y, core, across)

                @pl.when(valid)
                def _(index=index):
                    for half in range(parts):

                        @pl.when(needed(index, half))
                        def _(half=half):
                            arrived(index, half)
                            copy(index, half, SIBLING).start()

        if balanced:
            for way, here in inner_ways:

                for half in range(parts):

                    @pl.when((step == 1) & here & needed(partner, half))
                    def _(way=way, half=half):
                        copy(partner, half, way).start()

            for way, here in outer_ways:

                for half in late_halves:

                    @pl.when((step == 2) & here & needed(partner, half))
                    def _(way=way, half=half):
                        copy(partner, half, way).start()

        def visit(turn, inner):
            side = lax.rem(turn, 2)
            crossed = lax.rem(turn // 2, across)
            shared = turn // (2 * across)
            when = step - crossed - shared
            origin, valid = line(when, side)
            if across > 1:
                other_origin, other_valid = crossed_line(when, side)
                origin = jnp.where(crossed == 1, other_origin, origin)
                valid = ((crossed == 1) & other_valid) | ((crossed == 0) & valid)
            index = index_of(origin, lax.rem(y + crossed, across), lax.rem(core + shared, 2), across)

            @pl.when(valid)
            def _():
                for half in range(parts):

                    @pl.when((shared == 1) & needed(index, half))
                    def _(half=half):
                        arrived(index, half)

                use(index)

            return inner

        return lax.fori_loop(0, 4 * across, visit, carry) if use else carry

    lax.fori_loop(0, depth + across, body, 0)
    if not use:

        def collect(origin, carry):
            for there in range(across):
                index = index_of(origin, there, 1 - core, across)
                for half in range(parts):

                    @pl.when(needed(index, half))
                    def _(index=index, half=half):
                        arrived(index, half)

            return carry

        lax.fori_loop(0, depth, collect, 0)

    def settle(origin, carry):
        own = index_of(origin, y, core, across)
        for half in range(parts):

            wanted = needed(own, half)

            if direct:

                @pl.when(needed(me, half) & (origin != z))
                def _():
                    straight(origin, half).wait_send()

            else:

                @pl.when(wanted & (z < depth - 1) & (origin <= z))
                def _():
                    copy(own, half, UP).wait_send()

                @pl.when(wanted & (z > 0) & (origin >= z))
                def _():
                    copy(own, half, DOWN).wait_send()

            @pl.when(wanted)
            def _():
                copy(own, half, SIBLING).wait_send()

            if across > 1:

                @pl.when(wanted & crosses(origin, half))
                def _():
                    copy(own, half, ACROSS).wait_send()

                other = index_of(origin, 1 - y, core, across)

                @pl.when(needed(other, half))
                def _():
                    copy(other, half, SIBLING).wait_send()
        return carry

    lax.fori_loop(0, depth, settle, 0)
    if balanced:
        for way, here in inner_ways:

            for half in range(parts):

                @pl.when(here & needed(partner, half))
                def _(way=way, half=half):
                    copy(partner, half, way).wait_send()

        for way, here in outer_ways:

            for half in late_halves:

                @pl.when(here & needed(partner, half))
                def _(way=way, half=half):
                    copy(partner, half, way).wait_send()


def spread_partners(width):
    depth, across = layout(width)
    me = lax.axis_index("ind")
    z, y, core = place_of(me, across)
    partners = [
        (z < depth - 1, index_of(z + 1, y, core, across)),
        (z > 0, index_of(z - 1, y, core, across)),
        (z >= 0, index_of(z, y, 1 - core, across)),
    ]
    if across > 1:
        partners.append((z >= 0, index_of(z, 1 - y, core, across)))
    return partners


def gram_kernel(
    width, per_fold, genotypes_in, phenotypes_in, folds_in, total, own,
    blocks, send, receive, genotypes, phenotypes, folds, arrivals,
):
    me = lax.axis_index("ind")
    rows, size = total.shape[1], total.shape[0]
    fold = jnp.minimum(me // per_fold, FOLDS - 1).astype(jnp.float32)

    pairs = ((genotypes_in, genotypes), (phenotypes_in, phenotypes), (folds_in, folds))
    fills = [pltpu.make_async_copy(a, b, arrivals.at[i]) for i, (a, b) in enumerate(pairs)]
    for fill in fills:
        fill.start()

    def prepare():
        total[...] = jnp.zeros_like(total)
        for fill in fills:
            fill.wait()
        members = folds[...].astype(jnp.float32)
        block = jnp.concatenate(
            [
                genotypes[...].T,
                phenotypes[...],
                jnp.broadcast_to(members, (EXTRA, members.shape[1])).astype(jnp.bfloat16),
            ],
            axis=0,
        )
        blocks[me] = block
        own[...] = block

    greet(spread_partners(width), prepare)

    def use(index):
        keep = (blocks[index, rows : rows + EXTRA, :].astype(jnp.float32)[:1] != fold).astype(jnp.bfloat16)
        total[...] += lax.dot_general(
            blocks[index, :size, :] * keep,
            blocks[index, :rows, :],
            (((1,), (1,)), ((), ())),
            preferred_element_type=jnp.float32,
        )

    spread(blocks, send, receive, width, use, lambda index, half: index >= 0, False)


def leave_gram(genotypes, phenotypes, folds, width):
    individuals, size = genotypes.shape
    traits = phenotypes.shape[0]
    rows = size + traits + EXTRA
    per_fold, _ = plan(width)
    return pl.pallas_call(
        functools.partial(gram_kernel, width, per_fold),
        out_shape=(
            jax.ShapeDtypeStruct((size, size + traits), jnp.float32),
            jax.ShapeDtypeStruct((rows, individuals), jnp.bfloat16),
        ),
        in_specs=[pl.BlockSpec(memory_space=pl.ANY)] * 3,
        scratch_shapes=[
            pltpu.VMEM((width, rows, individuals), jnp.bfloat16),
            pltpu.SemaphoreType.DMA((4, width, PIECES)),
            pltpu.SemaphoreType.DMA((width, PIECES)),
            pltpu.VMEM(genotypes.shape, jnp.bfloat16),
            pltpu.VMEM(phenotypes.shape, jnp.bfloat16),
            pltpu.VMEM((1, individuals), jnp.int32),
            pltpu.SemaphoreType.DMA((3,)),
        ],
        compiler_params=pltpu.CompilerParams(
            collective_id=0,
            has_side_effects=True,
            vmem_limit_bytes=(15 << 20) + 2 * width * rows * individuals,
        ),
    )(genotypes, phenotypes, folds[None])


def small_solve(matrix, rhs):
    size = len(rhs)
    lower = {}
    for column in range(size):
        total = matrix[column][column]
        for inner in range(column):
            total = total - lower[column, inner] * lower[column, inner]
        lower[column, column] = jnp.sqrt(total)
        for row in range(column + 1, size):
            total = matrix[row][column]
            for inner in range(column):
                total = total - lower[row, inner] * lower[column, inner]
            lower[row, column] = total / lower[column, column]
    forward = []
    for row in range(size):
        total = rhs[row]
        for inner in range(row):
            total = total - lower[row, inner] * forward[inner]
        forward.append(total / lower[row, row])
    backward = {}
    for row in reversed(range(size)):
        total = forward[row]
        for inner in range(row + 1, size):
            total = total - lower[inner, row] * backward[inner]
        backward[row] = total / lower[row, row]
    return [backward[row] for row in range(size)]


def predict_kernel(
    width, per_fold, slots, ridges, system, block, raw, sums,
    work, coefficients, near, far, send, receive, near_send, near_receive, far_send, far_receive,
):
    size = coefficients.shape[2]
    traits = coefficients.shape[1] // slots
    rows = size + traits
    depth, across = layout(width)
    me = lax.axis_index("ind")
    z, y, core = place_of(me, across)
    corner = y * 2 + core
    near_devices = [(lax.rem(corner + k, 2 * across), k) for k in range(1, 2 * across)]
    far_devices = [(lax.rem(z + k, depth), k) for k in range(1, depth)]
    always = me >= 0
    geno = block[:size, :]
    phen = block[size:rows, :].astype(jnp.float32)
    folds = block[rows : rows + 1, :].astype(jnp.float32)

    def prepare():
        solve_systems(system, work, coefficients.at[me], ridges, slots, per_fold, me)

    greet(
        [(always, z * 2 * across + other) for other, _ in near_devices]
        + [(always, other * 2 * across + corner) for other, _ in far_devices],
        prepare,
    )
    cut = -(-slots * traits // 32) * 16

    def level_of(index, slot):
        return lax.rem(index, per_fold) * slots + slot

    def needed(index, half):
        return (index < FOLDS * per_fold) & (level_of(index, half * cut // traits) < RIDGES)

    spread(coefficients, send, receive, width, None, needed, True)
    total = None
    for fold in range(FOLDS):
        masked = geno * (folds == float(fold)).astype(jnp.bfloat16)
        flat = jnp.concatenate(
            [
                coefficients[fold * per_fold + r // slots, pl.ds(r % slots * traits, traits)]
                for r in range(RIDGES)
            ],
            axis=0,
        )
        part = lax.dot_general(flat, masked, (((1,), (0,)), ((), ())), preferred_element_type=jnp.float32)
        total = part if total is None else total + part
    raw[...] = total
    parts = [total[r * traits : (r + 1) * traits] for r in range(RIDGES)]
    lane = lax.broadcasted_iota(jnp.int32, (traits, TILE), 1)
    packed = jnp.zeros((traits, TILE), jnp.float32)
    place = 0
    for r in range(RIDGES):
        for other in parts[: r + 1] + [phen]:
            packed = jnp.where(lane == place, jnp.sum(parts[r] * other, axis=1, keepdims=True), packed)
            place += 1

    def exchange(buffer, mine, devices, sends, receives, device_of):
        copies = []
        for other, k in devices:
            copy = copy_to(
                buffer.at[mine], buffer.at[mine], sends.at[k], receives.at[mine], device_of(other)
            )
            copy.start()
            copies.append(copy)
        for other, k in devices:
            copy_to(
                buffer.at[other], buffer.at[other], sends.at[k], receives.at[other], device_of(other)
            ).wait_recv()
        for copy in copies:
            copy.wait_send()

    spare = jnp.zeros((SUMS, TILE - traits), jnp.float32)
    near[corner] = jnp.concatenate([packed.T[:SUMS], spare], axis=1)
    exchange(near, corner, near_devices, near_send, near_receive, lambda other: z * 2 * across + other)
    far[z] = jnp.sum(near[...], axis=0)
    exchange(far, z, far_devices, far_send, far_receive, lambda other: other * 2 * across + corner)
    gathered = jnp.sum(far[...], axis=0)
    filled = jnp.concatenate([gathered, jnp.zeros((TILE - SUMS, TILE), jnp.float32)], axis=0)
    sums[...] = filled.T[:traits]


def predict(system, own, ridges, width):
    size = system.shape[0]
    per_fold, slots = plan(width)
    traits = system.shape[1] - size
    depth, across = layout(width)
    return pl.pallas_call(
        functools.partial(predict_kernel, width, per_fold, slots, ridges),
        out_shape=(
            jax.ShapeDtypeStruct((RIDGES * traits, own.shape[1]), jnp.float32),
            jax.ShapeDtypeStruct((traits, TILE), jnp.float32),
        ),
        scratch_shapes=[
            pltpu.VMEM((slots, size, size + traits), jnp.float32),
            pltpu.VMEM((width, slots * traits, size), jnp.bfloat16),
            pltpu.VMEM((2 * across, SUMS, TILE), jnp.float32),
            pltpu.VMEM((depth, SUMS, TILE), jnp.float32),
            pltpu.SemaphoreType.DMA((4, width, 2)),
            pltpu.SemaphoreType.DMA((width, 2)),
            pltpu.SemaphoreType.DMA((2 * across,)),
            pltpu.SemaphoreType.DMA((2 * across,)),
            pltpu.SemaphoreType.DMA((depth,)),
            pltpu.SemaphoreType.DMA((depth,)),
        ],
        compiler_params=pltpu.CompilerParams(
            collective_id=1, has_side_effects=True, vmem_limit_bytes=40 << 20
        ),
    )(system, own)


def finish_kernel(count, ridges, sums, raw, block, stacked):
    traits = sums.shape[0]
    gram = {}
    cross = []
    place = 0
    for r in range(RIDGES):
        for s in range(r + 1):
            gram[r, s] = sums[:, place : place + 1]
            place += 1
        cross.append(sums[:, place : place + 1])
        place += 1
    scale = [1.0 / jnp.sqrt(gram[r, r] / count + epsilon) for r in range(RIDGES)]
    lane = lax.broadcasted_iota(jnp.int32, (traits, TILE), 1)
    ridge = jnp.full((traits, TILE), ridges[0], jnp.float32)
    for s in range(1, RIDGES):
        ridge = jnp.where(lane == s, ridges[s], ridge)
    matrix = [
        [
            jnp.broadcast_to(gram[r, s] * scale[r] * scale[s], (traits, TILE)) + (ridge if r == s else 0.0)
            if s <= r
            else None
            for s in range(RIDGES)
        ]
        for r in range(RIDGES)
    ]
    rhs = [jnp.broadcast_to(cross[r] * scale[r], (traits, TILE)) for r in range(RIDGES)]
    weights = small_solve(matrix, rhs)
    parts = []
    for r in range(RIDGES):
        part = raw[r * traits : (r + 1) * traits, :] * scale[r]
        block[r] = part
        parts.append(part)
    for s in range(RIDGES):
        total = weights[0][:, s : s + 1] * parts[0]
        for r in range(1, RIDGES):
            total = total + weights[r][:, s : s + 1] * parts[r]
        stacked[s] = total


def shards(genotypes, phenotypes, folds):
    rows = genotypes.shape[0]
    traits = phenotypes.shape[0]
    width = lax.axis_size("ind")
    count = rows * width
    ridges = ridge_list(count)
    total, own = leave_gram(genotypes, phenotypes, folds, width)
    raw, sums = predict(total, own, ridges, width)
    shape = jax.ShapeDtypeStruct((RIDGES, traits, rows), jnp.float32)
    return pl.pallas_call(
        functools.partial(finish_kernel, count, ridges),
        out_shape=(shape, shape),
        compiler_params=pltpu.CompilerParams(vmem_limit_bytes=40 << 20),
    )(sums, raw)


def solution(mesh):
    placed = (P(("cohort", "ind"), None), P(None, ("cohort", "ind")), P(("cohort", "ind")))
    return jax.shard_map(
        shards,
        mesh=mesh,
        in_specs=placed,
        out_specs=(P(None, None, ("cohort", "ind")), P(None, None, ("cohort", "ind"))),
        check_vma=False,
    )
```
